32 devices in a mesh: group: 2 (over x), row: 16 (over z, y, core).
Axes of the slice: x: 2, y: 2, z: 4, core: 2. Of those that a mesh axis runs over, the one named last changes fastest.
Arguments:
- base_currents: bfloat16 [32768, 1024], P(('group', 'row')), parts along dimension 0, may hold values from -6 to 6
- term_rows: bfloat16 [8192, 1024], P(('group', 'row')), parts along dimension 0, may hold values from -12 to 12
- term_owner: int32 [8192, 1], P(('group', 'row')), parts along dimension 0, may hold values from 0 to 15; in each aligned block of 256 rows (0 to 255, 256 to 511, ...) at most 32 rows name the same one
- term_slot: int32 [8192, 1], P(('group', 'row')), parts along dimension 0, may hold values from 0 to 1023
- inductance: bfloat16 [64, 20, 256, 256], P('row'), may hold values from -0.078125 to 0.078125
- block_cols: int32 [64, 20], P('row'), may hold values from 0 to 63, as said below
Outputs:
- flux: bfloat16 [32768, 1024], P(('group', 'row')), parts along dimension 0
The draws below stay inside these ranges and needn't reach their ends.
There are 2 independent parts, one for each index of `group`. The reference program is written for one: setup_inputs(seed, part) draws one part's arguments, and reference() takes and returns one part's arrays. A program takes and returns all parts, laid end to end along the dimension named above; an argument that names none is the same for every part. Nothing has to cross between parts.
Inputs may be any that keep to these rules, and one draw needn't show every extreme that they name: `block_cols`: the block rows of device i (block rows i * 4 to i * 4 + 3) list only block columns of devices i - 2 to i + 2; every block row lists a column of device max(i - 2, 0) and one of device min(i + 2, the last device). Columns may repeat. `term_owner`: among the 256 terminal rows of one device, at most 32 name the same owner, and that many is reached.
All inputs are finite; a program needn't handle non-finite values.
Results may differ from the reference program's by a relative error of at most 0.0046.
Values may be sent and summed in bfloat16 or wider, within the bound.
No kernel may reach another device: no remote copies, remote signals or barrier semaphores. Data moves between devices by JAX's collectives and lax.ppermute only.
A program may use at most 128 MiB of HBM per device.

```python
import math
import jax
import jax.numpy as jnp
import numpy as np
from jax import lax

BLOCK = 256
RB_DEV = 4
K = 20
HALO = 2
W = 1024
TERM_DEV = 256
CAP = 32
SEG_DEV = 1024
ORDER = 16384
BROWS = 64
TERMS = 4096
N_ROW = 16


def draw_block_cols(key, part):
    devices = BROWS // RB_DEV
    row_ids = jnp.arange(BROWS)
    home_dev = row_ids // RB_DEV
    lowest = jnp.maximum(home_dev - HALO, 0)
    highest = jnp.minimum(home_dev + HALO, devices - 1)
    key_owner = jax.random.fold_in(key, 11)
    key_within = jax.random.fold_in(key, 12)
    key_forced = jax.random.fold_in(key, 13)
    owner_dev = jax.random.randint(key_owner, (BROWS, K), lowest[:, None], highest[:, None] + 1)
    forced = jax.random.randint(key_forced, (BROWS, 1), 0, K)
    entry_ids = jnp.arange(K)[None, :]
    owner_dev = jnp.where(entry_ids == forced, lowest[:, None], owner_dev)
    owner_dev = jnp.where(entry_ids == (forced + 1) % K, highest[:, None], owner_dev)
    within = jax.random.randint(key_within, (BROWS, K), 0, RB_DEV)
    return (owner_dev * RB_DEV + within).astype(jnp.int32)


def touch_ends(entries, rng, least, top_value):
    index_at = [jax.random.randint(jax.random.fold_in(rng, axis), (), 0, length) for axis, length in enumerate(entries.shape)]
    main_axis = entries.shape.index(max(entries.shape))
    next_to = index_at[:main_axis] + [(index_at[main_axis] + 1) % entries.shape[main_axis]] + index_at[main_axis + 1:]
    return entries.at[tuple(index_at)].set(least).at[tuple(next_to)].set(top_value)


def level_of(key, extent, cuts, least, largest):
    def one(axis_at, parts):
        steps = jax.random.uniform(jax.random.fold_in(jax.random.fold_in(key, 6), axis_at), (parts,), jnp.float32, least / len(cuts), largest / len(cuts))
        return jnp.repeat(jnp.exp(steps), extent[axis_at] // parts).reshape((-1,) + (1,) * (len(extent) - axis_at - 1))

    factor_of = one(*cuts[0])
    for cut in cuts[1:]:
        factor_of = factor_of * one(*cut)
    return factor_of


def routed_block(rng, own, number, rows, count, top, bound, lean):
    order = jax.random.permutation(rng, count)
    heavy_load, usual = portions_of(count, rows * top, bound, lean, True), portions_of(count, rows * top, bound, lean, False)
    places = jnp.arange(count)

    def named(lengths, rotation):
        used = int((lengths > 0).sum())
        fixed = max(1, used // 4)
        shifted = fixed + (places - fixed + rotation * (used - fixed)) % max(1, count - fixed)
        return jnp.zeros((count,), jnp.int32).at[order[jnp.where(places < fixed, places, shifted)]].set(jnp.asarray(lengths, jnp.int32))

    lengths = jnp.where(number % 4 == 0, named(heavy_load, number // 4), named(usual, number - number // 4 - 1))
    mixed = jax.random.permutation(jax.random.fold_in(own, 3), count)
    source_of, taker = mixed[0:count // 2 * 2:2], mixed[1:count // 2 * 2:2]
    margin = jnp.minimum(lengths[source_of] - 1, bound - lengths[taker]) // 2
    margin = jnp.where((source_of == order[0]) | (taker == order[0]) | (lengths[taker] == 0), 0, jnp.maximum(margin, 0))
    shifted = jax.random.randint(jax.random.fold_in(own, 4), (count // 2,), 0, 1 << 20) % (margin + 1)
    lengths = lengths.at[source_of].add(-shifted).at[taker].add(shifted)
    members = jnp.searchsorted(jnp.cumsum(lengths), jnp.arange(rows * top), side="right").astype(jnp.int32)
    grid = members.reshape(top, rows).T
    grid = grid[jax.random.permutation(jax.random.fold_in(own, 1), rows)]
    rotation = jax.random.randint(jax.random.fold_in(own, 2), (rows, 1), 0, top)
    return jnp.take_along_axis(grid, (jnp.arange(top)[None, :] + rotation) % top, axis=1)


def portions_of(number_of, total, bound, skew, full):
    loads = [(1 << 20) // math.isqrt(rank ** skew) + 1 for rank in range(1, number_of + 1)]
    largest = bound if full else min(bound, max(-(-total // number_of), total * loads[0] // sum(loads)))
    least = 1 if total - largest >= number_of - 1 else 0
    counts, spare = [largest] + [least] * (number_of - 1), total - largest - least * (number_of - 1)
    while spare > 0:
        free = [i for i in range(1, number_of) if counts[i] < largest] or [i for i in range(1, number_of) if counts[i] < bound]
        pool, budget = sum([loads[i] for i in free]), spare
        for i in free:
            addition = min(bound - counts[i], max(1, budget * loads[i] // pool), spare)
            counts[i] = counts[i] + addition
            spare = spare - addition
    return np.array(counts)


def bell_draw(key, dims, width, reach, shards=(), kind=jnp.bfloat16):
    array = width * jax.random.normal(key, dims, jnp.float32)
    if shards:
        array = array * level_of(key, dims, shards, -0.22, 0.18)
    return jnp.clip(array, -reach, reach).astype(kind)


def setup_inputs(seed: int = 0, part: int = 0) -> dict:
    splits = jax.random.split(jax.random.key(seed), 7)
    own_keys = jax.random.split(jax.random.fold_in(splits[6], part), 7)
    base_currents = bell_draw(own_keys[0], (ORDER, W), 1.0, 6.0, ((0, 16),))
    term_rows = bell_draw(own_keys[1], (TERMS, W), 3.0, 12.0, ((0, 16),))
    term_owner_keys = jax.random.split(jax.random.fold_in(own_keys[2], 1), TERMS // TERM_DEV)
    term_owner_turns = jax.random.permutation(jax.random.fold_in(own_keys[2], 3), TERMS // TERM_DEV)
    term_owner = jax.vmap(lambda own, number: routed_block(jax.random.fold_in(own_keys[2], 2), own, number, TERM_DEV, N_ROW, 1, CAP, 2))(term_owner_keys, term_owner_turns).reshape((TERMS, 1))
    term_slot = touch_ends(jax.random.randint(own_keys[3], (TERMS, 1), 0, SEG_DEV), jax.random.fold_in(own_keys[3], 1), 0, SEG_DEV - 1).astype(jnp.int32)
    inductance = bell_draw(splits[4], (BROWS, K, BLOCK, BLOCK), (K * BLOCK) ** -0.5, 0.078125, ((0, 16),))
    block_cols = draw_block_cols(jax.random.fold_in(splits[6], 71), part)
    return {"base_currents": base_currents, "term_rows": term_rows, "term_owner": term_owner, "term_slot": term_slot, "inductance": inductance, "block_cols": block_cols}


def reference(base_currents, term_rows, term_owner, term_slot, inductance, block_cols):
    segment_of = (term_owner[:, 0] * SEG_DEV + term_slot[:, 0]).astype(jnp.int32)
    injected = jax.ops.segment_sum(term_rows.astype(jnp.float32), segment_of, num_segments=ORDER)
    currents = (base_currents.astype(jnp.float32) + injected).astype(jnp.bfloat16)
    current_blocks = currents.reshape(BROWS, BLOCK, W)

    def one_row(inputs):
        tiles, columns = inputs
        picked = current_blocks[columns.astype(jnp.int32)]
        return jnp.einsum("kab,kbw->aw", tiles.astype(jnp.float32), picked.astype(jnp.float32))

    linked = lax.map(one_row, (inductance, block_cols))
    return linked.reshape(ORDER, W).astype(jnp.bfloat16)
```

```python
import functools

import jax
import jax.numpy as jnp
from jax import lax
from jax.experimental import pallas as pl
from jax.experimental.pallas import tpu as pltpu
from jax.sharding import PartitionSpec as P

HALO = 2
AHEAD = 9
LANES = 128
RADIX = 32
VMEM = pl.BlockSpec(memory_space=pltpu.VMEM)
SMEM = pl.BlockSpec(memory_space=pltpu.SMEM)
HBM = pl.BlockSpec(memory_space=pltpu.HBM)
ANY = pl.BlockSpec(memory_space=pl.ANY)
SLOTS = 2 * HALO + 1
TOKEN = jax.ShapeDtypeStruct((8, LANES), jnp.float32)
MIB = 1024 * 1024


def limit(mib):
    return pltpu.CompilerParams(vmem_limit_bytes=mib * MIB)


def in_hbm(value):
    return pltpu.with_memory_space_constraint(value, pltpu.HBM)


def gate_kernel(*refs):
    pass


def gate(value, *others):
    return pl.pallas_call(
        gate_kernel,
        out_shape=pltpu.HBM(value.shape, value.dtype),
        in_specs=[HBM] + [ANY] * len(others),
        out_specs=HBM,
        input_output_aliases={0: 0},
        compiler_params=limit(1),
        name="gate",
    )(in_hbm(value), *others)


def column_cuts(width):
    unit = width // 8
    return [[2 * unit], [3 * unit], [3 * unit]]


def pack_kernel(capacity, owner_ref, target_ref, rows_ref, out_ref):
    count, width = rows_ref.shape
    slots = out_ref.shape[0]
    owner = owner_ref[...]
    target = target_ref[...]
    named = lax.broadcasted_iota(jnp.int32, (LANES, count), 0) == owner
    tri = lax.broadcasted_iota(jnp.int32, (count, count), 0) < lax.broadcasted_iota(
        jnp.int32, (count, count), 1
    )
    earlier = jnp.dot(
        named.astype(jnp.bfloat16), tri.astype(jnp.bfloat16), preferred_element_type=jnp.float32
    )
    order = jnp.sum(jnp.where(named, earlier, 0.0), axis=0, keepdims=True).astype(jnp.int32)
    position = owner * capacity + order
    picker = (lax.broadcasted_iota(jnp.int32, (slots, count), 0) == position).astype(jnp.bfloat16)
    line = lax.broadcasted_iota(jnp.int32, (LANES, count), 0)
    tags = jnp.where(line == 0, target // RADIX + 1, jnp.where(line == 1, target % RADIX, 0))
    tags = tags.astype(jnp.float32).astype(jnp.bfloat16)
    out_ref[:, :width] = jnp.dot(
        picker, rows_ref[...], preferred_element_type=jnp.float32
    ).astype(jnp.bfloat16)
    out_ref[:, width:] = lax.dot_general(
        picker, tags, (((1,), (1,)), ((), ())), preferred_element_type=jnp.float32
    ).astype(jnp.bfloat16)


def inject_kernel(offset, base_ref, arrived_ref, wait_ref, *out_refs):
    seg_dev = base_ref.shape[0]
    slots = arrived_ref.shape[0]
    width = arrived_ref.shape[1] - LANES
    pick_lane = lax.broadcasted_iota(jnp.int32, (8, LANES), 1)
    weights = jnp.where(pick_lane == 0, float(RADIX), jnp.where(pick_lane == 1, 1.0, 0.0))
    segment = lax.dot_general(
        weights.astype(jnp.bfloat16),
        arrived_ref[:, width:],
        (((1,), (1,)), ((), ())),
        preferred_element_type=jnp.float32,
    )[0:1].astype(jnp.int32) - RADIX
    landing = (lax.broadcasted_iota(jnp.int32, (seg_dev, slots), 0) == segment).astype(jnp.bfloat16)
    for out_ref in out_refs:
        there = slice(offset, offset + out_ref.shape[1])
        injected = jnp.dot(landing, arrived_ref[:, there], preferred_element_type=jnp.float32)
        out_ref[...] = (base_ref[:, there].astype(jnp.float32) + injected).astype(jnp.bfloat16)
        offset += out_ref.shape[1]


def dense_kernel(cols_ref, slot_ref, blocks_ref, wait_ref, out_ref, token_ref, total_ref):
    row = pl.program_id(0)
    count = blocks_ref.shape[1]
    block = blocks_ref.shape[2]
    per_dev = cols_ref.shape[0]
    places = total_ref.shape[0]
    total_ref[...] = jnp.zeros_like(total_ref)
    token_ref[...] = jnp.zeros_like(token_ref)

    def add(k, carry):
        local = cols_ref[row, k] - slot_ref[SLOTS]
        at = slot_ref[local // per_dev] * per_dev + local % per_dev
        total_ref[at] = total_ref[at] + blocks_ref[0, k].astype(jnp.float32)
        return carry

    lax.fori_loop(0, count, add, 0)
    for at in range(places):
        out_ref[:, at * block : (at + 1) * block] = total_ref[at].astype(jnp.bfloat16)


def link_kernel(offset, sizes, flag_ref, dense_ref, *refs):
    parts = [refs[6 * i : 6 * i + 6] for i in range(len(sizes))]
    out_ref, token_ref, matrix, window, total, result, mat_sems, sems, out_sem = refs[-9:]
    token_ref[...] = jnp.zeros_like(token_ref)
    seg_dev = dense_ref.shape[0]
    width = sum(sizes)
    starts = [sum(sizes[:i]) for i in range(len(sizes))]

    def copies(slot, which):
        return [
            pltpu.make_async_copy(
                part[which], window.at[slot, :, pl.ds(start, size)], sems.at[slot, i]
            )
            for i, (part, start, size) in enumerate(zip(parts, starts, sizes))
        ]

    def columns(slot):
        return pltpu.make_async_copy(
            dense_ref.at[:, pl.ds(slot * seg_dev, seg_dev)], matrix.at[slot], mat_sems.at[slot]
        )

    for slot in range(SLOTS):
        columns(slot).start()
        if slot == 3:
            @pl.when(flag_ref[0] == 0)
            def _():
                for copy in copies(3, 3):
                    copy.start()

            @pl.when(flag_ref[0] == 1)
            def _():
                for copy in copies(3, 5):
                    copy.start()
        else:
            for copy in copies(slot, slot):
                copy.start()

    for slot in range(SLOTS):
        columns(slot).wait()
        for copy in copies(slot, 0):
            copy.wait()
        part = jnp.dot(matrix[slot], window[slot], preferred_element_type=jnp.float32)
        if slot == 0:
            total[...] = part
        elif slot < SLOTS - 1:
            total[...] += part
        else:
            result[...] = (total[...] + part).astype(jnp.bfloat16)
    out = pltpu.make_async_copy(result, out_ref.at[:, pl.ds(offset, width)], out_sem)
    out.start()
    out.wait()


def shards(base_currents, term_rows, term_owner, term_slot, inductance, block_cols):
    devices = lax.axis_size("row")
    me = lax.axis_index("row")
    seg_dev, width = base_currents.shape
    capacity = max(2, 2 * term_rows.shape[0] // devices)
    slots = devices * capacity
    rows_dev, count, block, _ = inductance.shape

    core, side = me % 2, (me // 2) % 2
    across = [(i, i ^ 2) for i in range(devices)]
    partner = [(i, i ^ 1) for i in range(devices)]
    relay = [(i, i + 4) for i in range(devices - 4) if not i & 2]
    relay += [(i + 4, i) for i in range(devices - 4) if i & 2]

    def send(value, pairs):
        return lax.ppermute(value, "row", pairs)

    near = jnp.where(core == 0, 3, 1)
    far = jnp.where(core == 0, 1, 3)
    slot_of = jnp.stack(
        [
            jnp.where(side == 0, 4, 2),
            near,
            jnp.zeros_like(near),
            far,
            jnp.where(side == 0, 2, 4),
            (me - HALO) * rows_dev,
        ]
    ).astype(jnp.int32)
    flag = jnp.where(core == side, 1, 0).astype(jnp.int32).reshape(1)

    outgoing = pl.pallas_call(
        functools.partial(pack_kernel, capacity),
        out_shape=jax.ShapeDtypeStruct((slots, width + LANES), jnp.bfloat16),
        in_specs=[VMEM] * 3,
        out_specs=VMEM,
        compiler_params=limit(16),
        name="pack_terms",
    )(term_owner.reshape(1, -1), term_slot.reshape(1, -1), term_rows)
    arrived = lax.all_to_all(
        outgoing.reshape(devices, capacity, width + LANES), "row", split_axis=0, concat_axis=0, tiled=True
    ).reshape(slots, width + LANES)

    dense, dense_token = pl.pallas_call(
        dense_kernel,
        out_shape=(pltpu.HBM((seg_dev, SLOTS * seg_dev), jnp.bfloat16), TOKEN),
        grid=(rows_dev,),
        in_specs=[SMEM, SMEM, pl.BlockSpec((1, count, block, block), lambda r: (r, 0, 0, 0)), HBM],
        out_specs=(pl.BlockSpec((block, SLOTS * seg_dev), lambda r: (r, 0)), pl.BlockSpec(TOKEN.shape, lambda r: (0, 0))),
        scratch_shapes=[pltpu.VMEM((SLOTS * rows_dev, block, block), jnp.float32)],
        compiler_params=limit(24),
        cost_estimate=pl.CostEstimate(flops=0, bytes_accessed=2 * inductance.size * 2, transcendentals=0),
        name="dense_blocks",
    )(block_cols, slot_of, in_hbm(inductance), in_hbm(outgoing))


    groups = column_cuts(width)
    flat = [size for sizes in groups for size in sizes]
    def inject(offset, sizes):
        return pl.pallas_call(
            functools.partial(inject_kernel, offset),
            out_shape=[jax.ShapeDtypeStruct((seg_dev, size), jnp.bfloat16) for size in sizes],
            in_specs=[VMEM, VMEM, ANY],
            out_specs=[VMEM] * len(sizes),
            compiler_params=limit(24),
            name="inject_terms",
        )(base_currents, arrived, dense_token)

    currents = [*inject(0, flat)]
    peers = []
    for k, current in enumerate(currents):
        if k >= AHEAD:
            current = currents[k] = gate(current, peers[k - AHEAD])
        peers.append(send(current, across))
    passed = [send(peer, relay) for peer in peers]

    def gather(k, token):
        beyond = passed[k]
        if token is not None:
            beyond = gate(beyond, token)
        return [
            currents[k],
            send(currents[k], partner),
            peers[k],
            send(peers[k], partner),
            beyond,
            send(beyond, partner),
        ]

    def link(out, offset, sizes, parts):
        given = [out] if out is not None else []
        total = sum(sizes)
        return pl.pallas_call(
            functools.partial(link_kernel, offset, sizes),
            out_shape=(pltpu.HBM((seg_dev, width), jnp.bfloat16), TOKEN),
            in_specs=[SMEM, HBM] + [HBM] * (len(parts) + len(given)),
            out_specs=(HBM, VMEM),
            scratch_shapes=[
                pltpu.VMEM((SLOTS, seg_dev, seg_dev), jnp.bfloat16),
                pltpu.VMEM((SLOTS, seg_dev, total), jnp.bfloat16),
                pltpu.VMEM((seg_dev, total), jnp.float32),
                pltpu.VMEM((seg_dev, total), jnp.bfloat16),
                pltpu.SemaphoreType.DMA((SLOTS,)),
                pltpu.SemaphoreType.DMA((SLOTS, len(sizes))),
                pltpu.SemaphoreType.DMA,
            ],
            input_output_aliases={2 + len(parts): 0} if given else {},
            compiler_params=limit(40),
            cost_estimate=pl.CostEstimate(
                flops=2 * seg_dev * SLOTS * seg_dev * total, bytes_accessed=0, transcendentals=0
            ),
            name="link_flux",
        )(
            flag,
            in_hbm(dense),
            *[in_hbm(part) for part in parts + given],
        )

    out, token, offset, at = None, None, 0, 0
    for sizes in groups:
        parts = sum([gather(at + i, token) for i in range(len(sizes))], [])
        at += len(sizes)
        out, token = link(out, offset, sizes, parts)
        offset += sum(sizes)
    return out


def solution(mesh):
    placed = (
        P(("group", "row"), None),
        P(("group", "row"), None),
        P(("group", "row"), None),
        P(("group", "row"), None),
        P("row", None, None, None),
        P("row", None),
    )
    return jax.shard_map(
        shards, mesh=mesh, in_specs=placed, out_specs=P(("group", "row"), None), check_vma=False
    )
```

```python
import functools

import jax
import jax.numpy as jnp
from jax import lax
from jax.experimental import pallas as pl
from jax.experimental.pallas import tpu as pltpu
from jax.sharding import PartitionSpec as P

HALO = 2
LANES = 128
RADIX = 32
VMEM = pl.BlockSpec(memory_space=pltpu.VMEM)
SMEM = pl.BlockSpec(memory_space=pltpu.SMEM)
HBM = pl.BlockSpec(memory_space=pltpu.HBM)
ANY = pl.BlockSpec(memory_space=pl.ANY)
SLOTS = 2 * HALO + 1
TOKEN = jax.ShapeDtypeStruct((8, LANES), jnp.float32)
HANDS = 3
LATE = 1
MIB = 1024 * 1024


def limit(mib):
    return pltpu.CompilerParams(vmem_limit_bytes=mib * MIB)


def in_hbm(value):
    return pltpu.with_memory_space_constraint(value, pltpu.HBM)


def gate_kernel(*refs):
    pass


def gate(value, *others):
    return pl.pallas_call(
        gate_kernel,
        out_shape=jax.ShapeDtypeStruct(value.shape, value.dtype),
        in_specs=[ANY] * (1 + len(others)),
        out_specs=ANY,
        input_output_aliases={0: 0},
        compiler_params=limit(1),
        name="gate",
    )(value, *others)


def chunk_sizes(width):
    unit = width // 8
    return [2 * unit] * 4


def pack_kernel(capacity, owner_ref, target_ref, rows_ref, out_ref):
    count, width = rows_ref.shape
    slots = out_ref.shape[0]
    owner = owner_ref[...]
    target = target_ref[...]
    named = lax.broadcasted_iota(jnp.int32, (LANES, count), 0) == owner
    tri = lax.broadcasted_iota(jnp.int32, (count, count), 0) < lax.broadcasted_iota(
        jnp.int32, (count, count), 1
    )
    earlier = jnp.dot(
        named.astype(jnp.bfloat16), tri.astype(jnp.bfloat16), preferred_element_type=jnp.float32
    )
    order = jnp.sum(jnp.where(named, earlier, 0.0), axis=0, keepdims=True).astype(jnp.int32)
    position = owner * capacity + order
    picker = (lax.broadcasted_iota(jnp.int32, (slots, count), 0) == position).astype(jnp.bfloat16)
    line = lax.broadcasted_iota(jnp.int32, (LANES, count), 0)
    tags = jnp.where(line == 0, target // RADIX + 1, jnp.where(line == 1, target % RADIX, 0))
    tags = tags.astype(jnp.float32).astype(jnp.bfloat16)
    out_ref[:, :width] = jnp.dot(
        picker, rows_ref[...], preferred_element_type=jnp.float32
    ).astype(jnp.bfloat16)
    out_ref[:, width:] = lax.dot_general(
        picker, tags, (((1,), (1,)), ((), ())), preferred_element_type=jnp.float32
    ).astype(jnp.bfloat16)


def inject_kernel(base_ref, arrived_ref, wait_ref, whole_ref, *out_refs):
    offset = 0
    seg_dev = base_ref.shape[0]
    slots = arrived_ref.shape[0]
    width = arrived_ref.shape[1] - LANES
    pick_lane = lax.broadcasted_iota(jnp.int32, (8, LANES), 1)
    weights = jnp.where(pick_lane == 0, float(RADIX), jnp.where(pick_lane == 1, 1.0, 0.0))
    segment = lax.dot_general(
        weights.astype(jnp.bfloat16),
        arrived_ref[:, width:],
        (((1,), (1,)), ((), ())),
        preferred_element_type=jnp.float32,
    )[0:1].astype(jnp.int32) - RADIX
    landing = (lax.broadcasted_iota(jnp.int32, (seg_dev, slots), 0) == segment).astype(jnp.bfloat16)
    for out_ref in out_refs:
        there = slice(offset, offset + out_ref.shape[1])
        injected = jnp.dot(landing, arrived_ref[:, there], preferred_element_type=jnp.float32)
        current = (base_ref[:, there].astype(jnp.float32) + injected).astype(jnp.bfloat16)
        out_ref[...] = current
        whole_ref[:, there] = current
        offset += out_ref.shape[1]


def dense_kernel(cols_ref, slot_ref, blocks_ref, wait_ref, out_ref, token_ref, total_ref):
    row = pl.program_id(0)
    count = blocks_ref.shape[1]
    block = blocks_ref.shape[2]
    per_dev = cols_ref.shape[0]
    places = total_ref.shape[0]
    total_ref[...] = jnp.zeros_like(total_ref)
    token_ref[...] = jnp.zeros_like(token_ref)

    def add(k, carry):
        local = cols_ref[row, k] - slot_ref[SLOTS]
        at = slot_ref[local // per_dev] * per_dev + local % per_dev
        total_ref[at] = total_ref[at] + blocks_ref[0, k].astype(jnp.float32)
        return carry

    lax.fori_loop(0, count, add, 0)
    for at in range(places):
        out_ref[:, at * block : (at + 1) * block] = total_ref[at].astype(jnp.bfloat16)


def hand_kernel(sizes, flag_ref, *refs):
    count = len(sizes)
    peers, passed = refs[:count], refs[count : 2 * count]
    out_ref, sems = refs[-2:]

    def copies(sources):
        return [
            pltpu.make_async_copy(
                source, out_ref.at[:, pl.ds(sum(sizes[:i]), sizes[i])], sems.at[i]
            )
            for i, source in enumerate(sources)
        ]

    @pl.when(flag_ref[1] == 0)
    def _():
        for copy in copies(peers):
            copy.start()

    @pl.when(flag_ref[1] == 1)
    def _():
        for copy in copies(passed):
            copy.start()

    for copy in copies(peers):
        copy.wait()


class Slots:
    def __init__(self, dense_ref, slots, matrix, window, mat_sems, sems):
        self.dense, self.slots = dense_ref, slots
        self.matrix, self.window, self.mat_sems, self.sems = matrix, window, mat_sems, sems

    def copies(self, slot):
        depth = self.dense.shape[0]
        columns = self.dense.at[:, pl.ds(slot * depth, depth)]
        made = [pltpu.make_async_copy(columns, self.matrix.at[slot], self.mat_sems.at[slot])]
        start = 0
        for i, piece in enumerate(self.slots[slot]):
            target = self.window.at[slot, :, pl.ds(start, piece.shape[1])]
            made.append(pltpu.make_async_copy(piece, target, self.sems.at[slot, i]))
            start += piece.shape[1]
        return made, start

    def begin(self, slot):
        for copy in self.copies(slot)[0]:
            copy.start()

    def sum_into(self, total_ref):
        self.begin(0)
        self.begin(1)
        for slot in range(len(self.slots)):
            made, wide = self.copies(slot)
            for copy in made:
                copy.wait()
            if slot + 2 < len(self.slots):
                self.begin(slot + 2)
            part = jnp.dot(
                self.matrix[slot], self.window[slot, :, :wide], preferred_element_type=jnp.float32
            )
            if slot == 0:
                total_ref[...] = part
            else:
                total_ref[:, :wide] += part


def part_kernel(offset, counts, dense_ref, own, beside, *refs):
    total_ref, token_ref, matrix, window, mat_sems, sems = refs[-6:]
    token_ref[...] = jnp.zeros_like(token_ref)
    there = pl.ds(offset, total_ref.shape[1])
    slots = [[own.at[:, there]], [beside.at[:, there]]]
    at = 0
    for count in counts:
        slots.append(refs[at : at + count])
        at += count
    Slots(dense_ref, slots, matrix, window, mat_sems, sems).sum_into(total_ref)


def last_kernel(plan, flag_ref, dense_ref, *refs):
    count = sum(len(item["inputs"]) for item in plan)
    inputs, outs = refs[:count], refs[count:]
    out_ref, matrix, window, extra, sums, result, mat_sems, row_sems, extra_sems, sum_sems, out_sems = outs
    seg_dev = dense_ref.shape[0]

    def columns(at, slot):
        there = dense_ref.at[:, pl.ds(slot * seg_dev, seg_dev)]
        return pltpu.make_async_copy(there, matrix.at[at], mat_sems.at[at])

    chunks, at = [], 0
    for i, item in enumerate(plan):
        chunk = dict(item, at=pl.ds(item["start"], item["size"]))
        chunk["given"] = inputs[at : at + len(item["inputs"])]
        at += len(item["inputs"])
        chunks.append(chunk)

    def into(target, sem, source):
        return pltpu.make_async_copy(source, target, sem)

    def sum_of(i, chunk):
        there = pl.ds(chunk["sum_start"], chunk["size"])
        return into(sums.at[:, chunk["at"]], sum_sems.at[i], chunk["given"][0].at[:, there])

    def rows_of(i, chunk, source):
        return into(window.at[:, chunk["at"]], row_sems.at[i], source)

    def extra_of(i, chunk):
        return into(extra.at[:, chunk["at"]], extra_sems.at[i], chunk["given"][-1])

    def result_of(i, chunk):
        return into(out_ref.at[:, chunk["at"]], out_sems.at[i], result.at[:, chunk["at"]])

    def begin(i, chunk):
        sum_of(i, chunk).start()
        if chunk["handed"]:
            rows_of(i, chunk, chunk["given"][1].at[:, chunk["at"]]).start()
        else:
            @pl.when(flag_ref[0] == 0)
            def _():
                rows_of(i, chunk, chunk["given"][1]).start()

            @pl.when(flag_ref[0] == 1)
            def _():
                rows_of(i, chunk, chunk["given"][2]).start()

        if chunk["relayed"]:
            extra_of(i, chunk).start()

    columns(0, SLOTS - 1).start()
    begin(0, chunks[0])
    begin(1, chunks[1])
    columns(1, SLOTS - 2).start()
    columns(0, SLOTS - 1).wait()
    waited = False
    for i, chunk in enumerate(chunks):
        if i + 2 < len(chunks):
            begin(i + 2, chunks[i + 2])
        rows_of(i, chunk, out_ref.at[:, chunk["at"]]).wait()
        sum_of(i, chunk).wait()
        there = chunk["at"]
        total = sums[:, there] + jnp.dot(matrix[0], window[:, there], preferred_element_type=jnp.float32)
        if chunk["relayed"]:
            if not waited:
                columns(1, SLOTS - 2).wait()
                waited = True
            extra_of(i, chunk).wait()
            total += jnp.dot(matrix[1], extra[:, there], preferred_element_type=jnp.float32)
        result[:, there] = total.astype(jnp.bfloat16)
        result_of(i, chunk).start()
    for i, chunk in enumerate(chunks):
        result_of(i, chunk).wait()


def shards(base_currents, term_rows, term_owner, term_slot, inductance, block_cols):
    devices = lax.axis_size("row")
    me = lax.axis_index("row")
    seg_dev, width = base_currents.shape
    capacity = max(2, 2 * term_rows.shape[0] // devices)
    slots = devices * capacity
    rows_dev, count, block, _ = inductance.shape

    core, side = me % 2, (me // 2) % 2
    across = [(i, i ^ 2) for i in range(devices)]
    partner = [(i, i ^ 1) for i in range(devices)]
    relay = [(i, i + 4) for i in range(devices - 4) if not i & 2]
    relay += [(i + 4, i) for i in range(devices - 4) if i & 2]

    def send(value, pairs):
        return lax.ppermute(value, "row", pairs)

    near = jnp.where(core == 0, 4, 1)
    far = jnp.where(core == 0, 1, 4)
    slot_of = jnp.stack(
        [
            jnp.where(side == 0, 3, 2),
            near,
            jnp.zeros_like(near),
            far,
            jnp.where(side == 0, 2, 3),
            (me - HALO) * rows_dev,
        ]
    ).astype(jnp.int32)
    flag = jnp.stack([core == side, core != side]).astype(jnp.int32)

    outgoing = pl.pallas_call(
        functools.partial(pack_kernel, capacity),
        out_shape=jax.ShapeDtypeStruct((slots, width + LANES), jnp.bfloat16),
        in_specs=[VMEM] * 3,
        out_specs=VMEM,
        compiler_params=limit(16),
        name="pack_terms",
    )(term_owner.reshape(1, -1), term_slot.reshape(1, -1), term_rows)
    arrived = lax.all_to_all(
        outgoing.reshape(devices, capacity, width + LANES), "row", split_axis=0, concat_axis=0, tiled=True
    ).reshape(slots, width + LANES)

    dense, dense_token = pl.pallas_call(
        dense_kernel,
        out_shape=(pltpu.HBM((seg_dev, SLOTS * seg_dev), jnp.bfloat16), TOKEN),
        grid=(rows_dev,),
        in_specs=[SMEM, SMEM, pl.BlockSpec((1, count, block, block), lambda r: (r, 0, 0, 0)), HBM],
        out_specs=(pl.BlockSpec((block, SLOTS * seg_dev), lambda r: (r, 0)), pl.BlockSpec(TOKEN.shape, lambda r: (0, 0))),
        scratch_shapes=[pltpu.VMEM((SLOTS * rows_dev, block, block), jnp.float32)],
        compiler_params=limit(24),
        cost_estimate=pl.CostEstimate(flops=0, bytes_accessed=0, transcendentals=0),
        name="dense_blocks",
    )(block_cols, slot_of, in_hbm(inductance), in_hbm(outgoing))


    sizes = chunk_sizes(width)
    starts = [sum(sizes[:k]) for k in range(len(sizes))]
    whole, *currents = pl.pallas_call(
        inject_kernel,
        out_shape=[
            jax.ShapeDtypeStruct((seg_dev, wide), jnp.bfloat16) for wide in [width] + sizes
        ],
        in_specs=[VMEM, VMEM, ANY],
        out_specs=[VMEM] * (1 + len(sizes)),
        compiler_params=limit(24),
        name="inject_terms",
    )(base_currents, arrived, dense_token)

    def cost():
        return pl.CostEstimate(flops=0, bytes_accessed=0, transcendentals=0)

    beside = send(whole, partner)
    peers = [send(current, across) for current in currents]

    passed = [send(peer, relay) for peer in peers]

    def part(start, slots, after):
        wide = sum(piece.shape[1] for piece in slots[0])
        given = [dense, whole, beside] + [piece for slot in slots for piece in slot]
        most = max(len(slot) for slot in slots)
        count = 2 + len(slots)
        return pl.pallas_call(
            functools.partial(part_kernel, start, [len(slot) for slot in slots]),
            out_shape=(pltpu.HBM((seg_dev, wide), jnp.float32), TOKEN),
            in_specs=[HBM] * len(given) + [ANY] * len(after),
            out_specs=(VMEM, VMEM),
            scratch_shapes=[
                pltpu.VMEM((count, seg_dev, seg_dev), jnp.bfloat16),
                pltpu.VMEM((count, seg_dev, wide), jnp.bfloat16),
                pltpu.SemaphoreType.DMA((count,)),
                pltpu.SemaphoreType.DMA((count, most)),
            ],
            compiler_params=limit(32),
            cost_estimate=cost(),
            name="part_flux",
        )(*[in_hbm(item) for item in given], *after)

    first, token = part(0, [peers[:2], passed[:2]], [])
    hands = HANDS
    mine = pl.pallas_call(
        functools.partial(hand_kernel, sizes[:hands]),
        out_shape=jax.ShapeDtypeStruct((seg_dev, sum(sizes[:hands])), jnp.bfloat16),
        in_specs=[SMEM] + [HBM] * (2 * hands) + [ANY],
        out_specs=VMEM,
        scratch_shapes=[pltpu.SemaphoreType.DMA((hands,))],
        compiler_params=limit(8),
        cost_estimate=cost(),
        name="hand_over",
    )(flag, *[in_hbm(item) for item in peers[:hands] + passed[:hands]], token)
    handed = send(mine, partner)
    second, token = part(starts[2], [peers[2:]] + ([passed[2:3]] if LATE else []), [mine])
    beyond = gate(passed[3], token)
    plan, parts = [], []
    for k, size in enumerate(sizes):
        item = dict(start=starts[k], size=size, handed=k < hands)
        item["sum_start"] = starts[k] if k < 2 else starts[k] - starts[2]
        item["relayed"] = k == 3 or (k == 2 and not LATE)
        last = beyond if k == 3 else passed[k]
        item["inputs"] = [first if k < 2 else second]
        if k < hands:
            item["inputs"] += [handed]
        else:
            item["inputs"] += [send(peers[k], partner), send(last, partner)]
        if item["relayed"]:
            item["inputs"] += [last]
        parts += item["inputs"]
        plan.append(item)
    plan = [dict(item, inputs=[0] * len(item["inputs"])) for item in plan]
    return pl.pallas_call(
        functools.partial(last_kernel, plan),
        out_shape=pltpu.HBM((seg_dev, width), jnp.bfloat16),
        in_specs=[SMEM, HBM] + [ANY] * len(parts),
        out_specs=HBM,
        scratch_shapes=[
            pltpu.VMEM((2, seg_dev, seg_dev), jnp.bfloat16),
            pltpu.VMEM((seg_dev, width), jnp.bfloat16),
            pltpu.VMEM((seg_dev, width), jnp.bfloat16),
            pltpu.VMEM((seg_dev, width), jnp.float32),
            pltpu.VMEM((seg_dev, width), jnp.bfloat16),
            pltpu.SemaphoreType.DMA((2,)),
            pltpu.SemaphoreType.DMA((len(sizes),)),
            pltpu.SemaphoreType.DMA((len(sizes),)),
            pltpu.SemaphoreType.DMA((len(sizes),)),
            pltpu.SemaphoreType.DMA((len(sizes),)),
        ],
        compiler_params=limit(32),
        cost_estimate=cost(),
        name="last_flux",
    )(flag, in_hbm(dense), *[in_hbm(p) if p is first or p is second or p is handed else p for p in parts])


def solution(mesh):
    placed = (
        P(("group", "row"), None),
        P(("group", "row"), None),
        P(("group", "row"), None),
        P(("group", "row"), None),
        P("row", None, None, None),
        P("row", None),
    )
    return jax.shard_map(
        shards, mesh=mesh, in_specs=placed, out_specs=P(("group", "row"), None), check_vma=False
    )
```

```python
import functools

import jax
import jax.numpy as jnp
from jax import lax
from jax.experimental import pallas as pl
from jax.experimental.pallas import tpu as pltpu
from jax.sharding import PartitionSpec as P

HALO = 2
PIECES = 1
AHEAD = 3
LANES = 128
RADIX = 32
VMEM = pl.BlockSpec(memory_space=pltpu.VMEM)
SMEM = pl.BlockSpec(memory_space=pltpu.SMEM)
HBM = pl.BlockSpec(memory_space=pltpu.HBM)
ANY = pl.BlockSpec(memory_space=pl.ANY)
SLOTS = 2 * HALO + 1
TOKEN = jax.ShapeDtypeStruct((8, LANES), jnp.float32)
WAIT = ('y3', 'z2')
GATE = True
MIB = 1024 * 1024


def limit(mib):
    return pltpu.CompilerParams(vmem_limit_bytes=mib * MIB)


def in_hbm(value):
    return pltpu.with_memory_space_constraint(value, pltpu.HBM)


def gate_kernel(*refs):
    pass


def gate(value, *others):
    return pl.pallas_call(
        gate_kernel,
        out_shape=jax.ShapeDtypeStruct(value.shape, value.dtype),
        in_specs=[ANY] * (1 + len(others)),
        out_specs=ANY,
        input_output_aliases={0: 0},
        compiler_params=limit(1),
        name="gate",
    )(value, *others)


def chunk_sizes(width):
    unit = width // 8
    return [2 * unit] * 4


def pack_kernel(capacity, owner_hbm, target_hbm, rows_hbm, out_ref, owner_ref, target_ref, rows_ref, sems):
    copies = [
        pltpu.make_async_copy(source, target, sems.at[i])
        for i, (source, target) in enumerate(
            [(owner_hbm, owner_ref), (target_hbm, target_ref), (rows_hbm, rows_ref)]
        )
    ]
    for copy in copies:
        copy.start()
    count, width = rows_ref.shape
    slots = out_ref.shape[0]
    tri = lax.broadcasted_iota(jnp.int32, (count, count), 0) < lax.broadcasted_iota(
        jnp.int32, (count, count), 1
    )
    line = lax.broadcasted_iota(jnp.int32, (LANES, count), 0)
    copies[0].wait()
    copies[1].wait()
    owner = owner_ref[...]
    target = target_ref[...]
    named = line == owner
    earlier = jnp.dot(
        named.astype(jnp.bfloat16), tri.astype(jnp.bfloat16), preferred_element_type=jnp.float32
    )
    order = jnp.sum(jnp.where(named, earlier, 0.0), axis=0, keepdims=True).astype(jnp.int32)
    position = owner * capacity + order
    picker = (lax.broadcasted_iota(jnp.int32, (slots, count), 0) == position).astype(jnp.bfloat16)
    tags = jnp.where(line == 0, target // RADIX + 1, jnp.where(line == 1, target % RADIX, 0))
    tags = tags.astype(jnp.float32).astype(jnp.bfloat16)
    out_ref[:, width:] = lax.dot_general(
        picker, tags, (((1,), (1,)), ((), ())), preferred_element_type=jnp.float32
    ).astype(jnp.bfloat16)
    copies[2].wait()
    out_ref[:, :width] = jnp.dot(
        picker, rows_ref[...], preferred_element_type=jnp.float32
    ).astype(jnp.bfloat16)


def inject_kernel(base_ref, arrived_ref, wait_ref, whole_ref, *out_refs):
    offset = 0
    seg_dev = base_ref.shape[0]
    slots = arrived_ref.shape[0]
    width = arrived_ref.shape[1] - LANES
    pick_lane = lax.broadcasted_iota(jnp.int32, (8, LANES), 1)
    weights = jnp.where(pick_lane == 0, float(RADIX), jnp.where(pick_lane == 1, 1.0, 0.0))
    segment = lax.dot_general(
        weights.astype(jnp.bfloat16),
        arrived_ref[:, width:],
        (((1,), (1,)), ((), ())),
        preferred_element_type=jnp.float32,
    )[0:1].astype(jnp.int32) - RADIX
    landing = (lax.broadcasted_iota(jnp.int32, (seg_dev, slots), 0) == segment).astype(jnp.bfloat16)
    for out_ref in out_refs:
        there = slice(offset, offset + out_ref.shape[1])
        injected = jnp.dot(landing, arrived_ref[:, there], preferred_element_type=jnp.float32)
        current = (base_ref[:, there].astype(jnp.float32) + injected).astype(jnp.bfloat16)
        out_ref[...] = current
        whole_ref[:, there] = current
        offset += out_ref.shape[1]


def dense_kernel(cols_ref, slot_ref, blocks_ref, wait_ref, out_ref, token_ref, total_ref):
    row = pl.program_id(0)
    count = blocks_ref.shape[1]
    block = blocks_ref.shape[2]
    per_dev = cols_ref.shape[0]
    places = total_ref.shape[0]
    total_ref[...] = jnp.zeros_like(total_ref)
    token_ref[...] = jnp.zeros_like(token_ref)

    def add(k, carry):
        local = cols_ref[row, k] - slot_ref[SLOTS]
        at = slot_ref[local // per_dev] * per_dev + local % per_dev
        total_ref[at] = total_ref[at] + blocks_ref[0, k].astype(jnp.float32)
        return carry

    lax.fori_loop(0, count, add, 0)
    for at in range(places):
        out_ref[:, at * block : (at + 1) * block] = total_ref[at].astype(jnp.bfloat16)


def hand_kernel(count, flag_ref, *refs):
    peers, passed = refs[:count], refs[count : 2 * count]
    out_refs, sems = refs[-1 - count * PIECES : -1], refs[-1]

    def copies(sources):
        made = []
        for i, out_ref in enumerate(out_refs):
            size = out_ref.shape[1]
            source = sources[i // PIECES].at[:, pl.ds(i % PIECES * size, size)]
            made.append(pltpu.make_async_copy(source, out_ref, sems.at[i]))
        return made

    @pl.when(flag_ref[1] == 0)
    def _():
        for copy in copies(peers):
            copy.start()

    @pl.when(flag_ref[1] == 1)
    def _():
        for copy in copies(passed):
            copy.start()

    for copy in copies(peers):
        copy.wait()


class Slots:
    def __init__(self, flag, dense_ref, slots, matrix, window, mat_sems, sems):
        self.flag, self.dense, self.slots = flag, dense_ref, slots
        self.matrix, self.window, self.mat_sems, self.sems = matrix, window, mat_sems, sems

    def columns(self, slot):
        depth = self.dense.shape[0]
        there = self.dense.at[:, pl.ds(slot * depth, depth)]
        return pltpu.make_async_copy(there, self.matrix.at[slot], self.mat_sems.at[slot])

    def rows(self, slot, i, piece):
        size = piece.shape[1]
        target = self.window.at[slot, :, pl.ds(i * size, size)]
        return pltpu.make_async_copy(piece, target, self.sems.at[slot, i])

    def begin(self, slot):
        self.columns(slot).start()
        for i, piece in enumerate(self.slots[slot]):
            if not isinstance(piece, tuple):
                self.rows(slot, i, piece).start()
                continue
            for value in range(2):
                @pl.when(self.flag == value)
                def _(value=value):
                    self.rows(slot, i, piece[value]).start()

    def sum_into(self, total_ref):
        for slot in range(AHEAD):
            self.begin(slot)
        last = len(self.slots) - 1
        for slot, pieces in enumerate(self.slots):
            self.columns(slot).wait()
            for i, piece in enumerate(pieces):
                self.rows(slot, i, piece[0] if isinstance(piece, tuple) else piece).wait()
            if slot + AHEAD <= last:
                self.begin(slot + AHEAD)
            part = jnp.dot(self.matrix[slot], self.window[slot], preferred_element_type=jnp.float32)
            if slot == 0:
                total_ref[...] = part
            elif slot < last:
                total_ref[...] += part
        return total_ref[...] + part


def flux_kernel(offset, count, paired, flag_ref, dense_ref, own, beside, *refs):
    out_ref, token_ref, matrix, window, total, result, mat_sems, sems, out_sem = refs[-9:]
    token_ref[...] = jnp.zeros_like(token_ref)
    there = pl.ds(offset, total.shape[1])
    peers, passed = refs[:count], refs[count : 2 * count]
    slots = [[own.at[:, there]], [beside.at[:, there]], peers, passed]
    if paired:
        slots.append(list(zip(refs[2 * count : 3 * count], refs[3 * count : 4 * count])))
    else:
        slots.append(refs[2 * count : 2 * count + count * PIECES])
    parts = Slots(flag_ref[0], dense_ref, slots, matrix, window, mat_sems, sems).sum_into(total)
    result[...] = parts.astype(jnp.bfloat16)
    out = pltpu.make_async_copy(result, out_ref.at[:, there], out_sem)
    out.start()
    out.wait()


def shards(base_currents, term_rows, term_owner, term_slot, inductance, block_cols):
    devices = lax.axis_size("row")
    me = lax.axis_index("row")
    seg_dev, width = base_currents.shape
    capacity = max(2, 2 * term_rows.shape[0] // devices)
    slots = devices * capacity
    rows_dev, count, block, _ = inductance.shape

    core, side = me % 2, (me // 2) % 2
    across = [(i, i ^ 2) for i in range(devices)]
    partner = [(i, i ^ 1) for i in range(devices)]
    relay = [(i, i + 4) for i in range(devices - 4) if not i & 2]
    relay += [(i + 4, i) for i in range(devices - 4) if i & 2]

    def send(value, pairs):
        return lax.ppermute(value, "row", pairs)

    near = jnp.where(core == 0, 4, 1)
    far = jnp.where(core == 0, 1, 4)
    slot_of = jnp.stack(
        [
            jnp.where(side == 0, 3, 2),
            near,
            jnp.zeros_like(near),
            far,
            jnp.where(side == 0, 2, 3),
            (me - HALO) * rows_dev,
        ]
    ).astype(jnp.int32)
    flag = jnp.stack([core == side, core != side]).astype(jnp.int32)

    outgoing = pl.pallas_call(
        functools.partial(pack_kernel, capacity),
        out_shape=jax.ShapeDtypeStruct((slots, width + LANES), jnp.bfloat16),
        in_specs=[HBM] * 3,
        out_specs=VMEM,
        scratch_shapes=[
            pltpu.VMEM((1, term_rows.shape[0]), jnp.int32),
            pltpu.VMEM((1, term_rows.shape[0]), jnp.int32),
            pltpu.VMEM(term_rows.shape, jnp.bfloat16),
            pltpu.SemaphoreType.DMA((3,)),
        ],
        compiler_params=limit(16),
        name="pack_terms",
    )(*[in_hbm(item) for item in (term_owner.reshape(1, -1), term_slot.reshape(1, -1), term_rows)])
    arrived = lax.all_to_all(
        outgoing.reshape(devices, capacity, width + LANES), "row", split_axis=0, concat_axis=0, tiled=True
    ).reshape(slots, width + LANES)

    dense, dense_token = pl.pallas_call(
        dense_kernel,
        out_shape=(pltpu.HBM((seg_dev, SLOTS * seg_dev), jnp.bfloat16), TOKEN),
        grid=(rows_dev,),
        in_specs=[SMEM, SMEM, pl.BlockSpec((1, count, block, block), lambda r: (r, 0, 0, 0)), HBM],
        out_specs=(pl.BlockSpec((block, SLOTS * seg_dev), lambda r: (r, 0)), pl.BlockSpec(TOKEN.shape, lambda r: (0, 0))),
        scratch_shapes=[pltpu.VMEM((SLOTS * rows_dev, block, block), jnp.float32)],
        compiler_params=limit(24),
        cost_estimate=pl.CostEstimate(flops=0, bytes_accessed=0, transcendentals=0),
        name="dense_blocks",
    )(block_cols, slot_of, in_hbm(inductance), in_hbm(outgoing))


    sizes = chunk_sizes(width)
    starts = [sum(sizes[:k]) for k in range(len(sizes))]
    whole, *currents = pl.pallas_call(
        inject_kernel,
        out_shape=[
            jax.ShapeDtypeStruct((seg_dev, wide), jnp.bfloat16) for wide in [width] + sizes
        ],
        in_specs=[VMEM, VMEM, ANY],
        out_specs=[VMEM] * (1 + len(sizes)),
        compiler_params=limit(24),
        name="inject_terms",
    )(base_currents, arrived, dense_token)

    def cost():
        return pl.CostEstimate(flops=0, bytes_accessed=0, transcendentals=0)

    beside = send(whole, partner)
    peers = [send(current, across) for current in currents]

    passed = [send(peer, relay) for peer in peers]

    size = sizes[0]
    half = len(sizes) // 2
    out_type = pltpu.HBM((seg_dev, width), jnp.bfloat16)

    def flux(start, chunks, others, paired, out, after=()):
        given = [dense, whole, beside] + peers[chunks] + passed[chunks] + others + out
        return pl.pallas_call(
            functools.partial(flux_kernel, start, half, paired),
            out_shape=(out_type, TOKEN),
            in_specs=[SMEM]
            + [ANY if start and any(item is other for other in others) else HBM for item in given]
            + [HBM] * len(after),
            out_specs=(HBM, VMEM),
            scratch_shapes=[
                pltpu.VMEM((SLOTS, seg_dev, seg_dev), jnp.bfloat16),
                pltpu.VMEM((SLOTS, seg_dev, half * size), jnp.bfloat16),
                pltpu.VMEM((seg_dev, half * size), jnp.float32),
                pltpu.VMEM((seg_dev, half * size), jnp.bfloat16),
                pltpu.SemaphoreType.DMA((SLOTS,)),
                pltpu.SemaphoreType.DMA((SLOTS, half * PIECES)),
                pltpu.SemaphoreType.DMA,
            ],
            input_output_aliases={len(given): 0} if out else {},
            compiler_params=limit(36),
            cost_estimate=cost(),
            name="flux",
        )(flag, *[in_hbm(item) if start == 0 or not any(item is other for other in others) else item for item in (*given, *after)])

    across_beside = [send(peer, partner) for peer in peers]
    passed_beside = [send(item, partner) for item in passed[:3]]
    others = across_beside[:half] + passed_beside[:half]
    out, token = flux(0, slice(0, half), others, True, [], [passed_beside[2]])
    passed[3] = gate(passed[3], token)
    passed_beside.append(send(passed[3], partner))
    others = across_beside[half:] + passed_beside[half:]
    out, _ = flux(half * size, slice(half, 2 * half), others, True, [out])
    return out


def solution(mesh):
    placed = (
        P(("group", "row"), None),
        P(("group", "row"), None),
        P(("group", "row"), None),
        P(("group", "row"), None),
        P("row", None, None, None),
        P("row", None),
    )
    return jax.shard_map(
        shards, mesh=mesh, in_specs=placed, out_specs=P(("group", "row"), None), check_vma=False
    )
```

```python
import functools

import jax
import jax.numpy as jnp
from jax import lax
from jax.experimental import pallas as pl
from jax.experimental.pallas import tpu as pltpu
from jax.sharding import PartitionSpec as P

HALO = 2
PIECES = 1
AHEAD = 3
SIGN = 2
LANES = 128
RADIX = 32
VMEM = pl.BlockSpec(memory_space=pltpu.VMEM)
SMEM = pl.BlockSpec(memory_space=pltpu.SMEM)
HBM = pl.BlockSpec(memory_space=pltpu.HBM)
ANY = pl.BlockSpec(memory_space=pl.ANY)
SLOTS = 2 * HALO + 1
TOKEN = jax.ShapeDtypeStruct((8, LANES), jnp.float32)
WAIT = ('y3', 'z2')
GATE = True
MIB = 1024 * 1024


def limit(mib):
    return pltpu.CompilerParams(vmem_limit_bytes=mib * MIB)


def in_hbm(value):
    return pltpu.with_memory_space_constraint(value, pltpu.HBM)


def gate_kernel(*refs):
    pass


def gate(value, *others):
    return pl.pallas_call(
        gate_kernel,
        out_shape=jax.ShapeDtypeStruct(value.shape, value.dtype),
        in_specs=[ANY] * (1 + len(others)),
        out_specs=ANY,
        input_output_aliases={0: 0},
        compiler_params=limit(1),
        name="gate",
    )(value, *others)


def chunk_sizes(width):
    unit = width // 8
    return [2 * unit, 2 * unit, 2 * unit, 2 * unit]


def pack_kernel(capacity, owner_hbm, target_hbm, rows_hbm, out_ref, owner_ref, target_ref, rows_ref, sems):
    copies = [
        pltpu.make_async_copy(source, target, sems.at[i])
        for i, (source, target) in enumerate(
            [(owner_hbm, owner_ref), (target_hbm, target_ref), (rows_hbm, rows_ref)]
        )
    ]
    for copy in copies:
        copy.start()
    count, width = rows_ref.shape
    slots = out_ref.shape[0]
    tri = lax.broadcasted_iota(jnp.int32, (count, count), 0) < lax.broadcasted_iota(
        jnp.int32, (count, count), 1
    )
    line = lax.broadcasted_iota(jnp.int32, (LANES, count), 0)
    copies[0].wait()
    copies[1].wait()
    owner = owner_ref[...]
    target = target_ref[...]
    named = line == owner
    earlier = jnp.dot(
        named.astype(jnp.bfloat16), tri.astype(jnp.bfloat16), preferred_element_type=jnp.float32
    )
    order = jnp.sum(jnp.where(named, earlier, 0.0), axis=0, keepdims=True).astype(jnp.int32)
    position = owner * capacity + order
    picker = (lax.broadcasted_iota(jnp.int32, (slots, count), 0) == position).astype(jnp.bfloat16)
    tags = jnp.where(line == 0, target // RADIX + 1, jnp.where(line == 1, target % RADIX, 0))
    tags = tags.astype(jnp.float32).astype(jnp.bfloat16)
    out_ref[:, width:] = lax.dot_general(
        picker, tags, (((1,), (1,)), ((), ())), preferred_element_type=jnp.float32
    ).astype(jnp.bfloat16)
    copies[2].wait()
    out_ref[:, :width] = jnp.dot(
        picker, rows_ref[...], preferred_element_type=jnp.float32
    ).astype(jnp.bfloat16)


def inject_kernel(base_ref, arrived_ref, wait_ref, whole_ref, *out_refs):
    offset = 0
    seg_dev = base_ref.shape[0]
    slots = arrived_ref.shape[0]
    width = arrived_ref.shape[1] - LANES
    pick_lane = lax.broadcasted_iota(jnp.int32, (8, LANES), 1)
    weights = jnp.where(pick_lane == 0, float(RADIX), jnp.where(pick_lane == 1, 1.0, 0.0))
    segment = lax.dot_general(
        weights.astype(jnp.bfloat16),
        arrived_ref[:, width:],
        (((1,), (1,)), ((), ())),
        preferred_element_type=jnp.float32,
    )[0:1].astype(jnp.int32) - RADIX
    landing = (lax.broadcasted_iota(jnp.int32, (seg_dev, slots), 0) == segment).astype(jnp.bfloat16)
    for out_ref in out_refs:
        there = slice(offset, offset + out_ref.shape[1])
        injected = jnp.dot(landing, arrived_ref[:, there], preferred_element_type=jnp.float32)
        current = (base_ref[:, there].astype(jnp.float32) + injected).astype(jnp.bfloat16)
        out_ref[...] = current
        whole_ref[:, there] = current
        offset += out_ref.shape[1]


def dense_kernel(cols_ref, slot_ref, blocks_ref, wait_ref, out_ref, token_ref, total_ref):
    row = pl.program_id(0)
    count = blocks_ref.shape[1]
    block = blocks_ref.shape[2]
    per_dev = cols_ref.shape[0]
    places = total_ref.shape[0]
    total_ref[...] = jnp.zeros_like(total_ref)
    token_ref[...] = jnp.zeros_like(token_ref)

    def add(k, carry):
        local = cols_ref[row, k] - slot_ref[SLOTS]
        at = slot_ref[local // per_dev] * per_dev + local % per_dev
        total_ref[at] = total_ref[at] + blocks_ref[0, k].astype(jnp.float32)
        return carry

    lax.fori_loop(0, count, add, 0)
    for at in range(places):
        out_ref[:, at * block : (at + 1) * block] = total_ref[at].astype(jnp.bfloat16)


def hand_kernel(count, flag_ref, *refs):
    peers, passed = refs[:count], refs[count : 2 * count]
    out_refs, sems = refs[-1 - count * PIECES : -1], refs[-1]

    def copies(sources):
        made = []
        for i, out_ref in enumerate(out_refs):
            size = out_ref.shape[1]
            source = sources[i // PIECES].at[:, pl.ds(i % PIECES * size, size)]
            made.append(pltpu.make_async_copy(source, out_ref, sems.at[i]))
        return made

    @pl.when(flag_ref[1] == 0)
    def _():
        for copy in copies(peers):
            copy.start()

    @pl.when(flag_ref[1] == 1)
    def _():
        for copy in copies(passed):
            copy.start()

    for copy in copies(peers):
        copy.wait()


class Slots:
    def __init__(self, flag, dense_ref, slots, matrix, window, mat_sems, sems):
        self.flag, self.dense, self.slots = flag, dense_ref, slots
        self.matrix, self.window, self.mat_sems, self.sems = matrix, window, mat_sems, sems

    def block(self, slot):
        depth = self.dense.shape[0]
        if self.matrix is None:
            return self.dense[:, slot * depth : (slot + 1) * depth]
        self.columns(slot).wait()
        return self.matrix[slot]

    def columns(self, slot):
        depth = self.dense.shape[0]
        there = self.dense.at[:, pl.ds(slot * depth, depth)]
        return pltpu.make_async_copy(there, self.matrix.at[slot], self.mat_sems.at[slot])

    def rows(self, slot, i, piece):
        before = [item[0] if isinstance(item, tuple) else item for item in self.slots[slot][:i]]
        start = sum(item.shape[1] for item in before)
        target = self.window.at[slot, :, pl.ds(start, piece.shape[1])]
        return pltpu.make_async_copy(piece, target, self.sems.at[slot, i])

    def begin(self, slot):
        if self.matrix is not None:
            self.columns(slot).start()
        for i, piece in enumerate(self.slots[slot]):
            if not isinstance(piece, tuple):
                self.rows(slot, i, piece).start()
                continue
            for value in range(2):
                @pl.when(self.flag == value)
                def _(value=value):
                    self.rows(slot, i, piece[value]).start()

    def sum_into(self, total_ref):
        for slot in range(AHEAD):
            self.begin(slot)
        last = len(self.slots) - 1
        for slot, pieces in enumerate(self.slots):
            for i, piece in enumerate(pieces):
                self.rows(slot, i, piece[0] if isinstance(piece, tuple) else piece).wait()
            if slot + AHEAD <= last:
                self.begin(slot + AHEAD)
            part = jnp.dot(self.block(slot), self.window[slot], preferred_element_type=jnp.float32)
            if slot == 0:
                total_ref[...] = part
            elif slot < last:
                total_ref[...] += part
        return total_ref[...] + part


def flux_kernel(offset, count, paired, flag_ref, dense_ref, own, beside, *refs):
    out_ref, token_ref, matrix, window, total, result, mat_sems, sems, out_sem = refs[-9:]
    token_ref[...] = jnp.zeros_like(token_ref)
    if offset:
        matrix = None
    there = pl.ds(offset, total.shape[1])
    peers, passed = refs[:count], refs[count : 2 * count]
    slots = [[own.at[:, there]], [beside.at[:, there]], peers, passed]
    if paired:
        slots.append(list(zip(refs[2 * count : 3 * count], refs[3 * count : 4 * count])))
    else:
        slots.append(refs[2 * count : 2 * count + count * PIECES])
    parts = Slots(flag_ref[0], dense_ref, slots, matrix, window, mat_sems, sems).sum_into(total)
    result[...] = parts.astype(jnp.bfloat16)
    out = pltpu.make_async_copy(result, out_ref.at[:, there], out_sem)
    out.start()
    out.wait()


def shards(base_currents, term_rows, term_owner, term_slot, inductance, block_cols):
    devices = lax.axis_size("row")
    me = lax.axis_index("row")
    seg_dev, width = base_currents.shape
    capacity = max(2, 2 * term_rows.shape[0] // devices)
    slots = devices * capacity
    rows_dev, count, block, _ = inductance.shape

    core, side = me % 2, (me // 2) % 2
    across = [(i, i ^ 2) for i in range(devices)]
    partner = [(i, i ^ 1) for i in range(devices)]
    relay = [(i, i + 4) for i in range(devices - 4) if not i & 2]
    relay += [(i + 4, i) for i in range(devices - 4) if i & 2]

    def send(value, pairs):
        return lax.ppermute(value, "row", pairs)

    near = jnp.where(core == 0, 4, 1)
    far = jnp.where(core == 0, 1, 4)
    slot_of = jnp.stack(
        [
            jnp.where(side == 0, 3, 2),
            near,
            jnp.zeros_like(near),
            far,
            jnp.where(side == 0, 2, 3),
            (me - HALO) * rows_dev,
        ]
    ).astype(jnp.int32)
    flag = jnp.stack([core == side, core != side]).astype(jnp.int32)

    outgoing = pl.pallas_call(
        functools.partial(pack_kernel, capacity),
        out_shape=jax.ShapeDtypeStruct((slots, width + LANES), jnp.bfloat16),
        in_specs=[HBM] * 3,
        out_specs=VMEM,
        scratch_shapes=[
            pltpu.VMEM((1, term_rows.shape[0]), jnp.int32),
            pltpu.VMEM((1, term_rows.shape[0]), jnp.int32),
            pltpu.VMEM(term_rows.shape, jnp.bfloat16),
            pltpu.SemaphoreType.DMA((3,)),
        ],
        compiler_params=limit(16),
        name="pack_terms",
    )(*[in_hbm(item) for item in (term_owner.reshape(1, -1), term_slot.reshape(1, -1), term_rows)])
    arrived = lax.all_to_all(
        outgoing.reshape(devices, capacity, width + LANES), "row", split_axis=0, concat_axis=0, tiled=True
    ).reshape(slots, width + LANES)

    dense, dense_token = pl.pallas_call(
        dense_kernel,
        out_shape=(pltpu.HBM((seg_dev, SLOTS * seg_dev), jnp.bfloat16), TOKEN),
        grid=(rows_dev,),
        in_specs=[SMEM, SMEM, pl.BlockSpec((1, count, block, block), lambda r: (r, 0, 0, 0)), HBM],
        out_specs=(pl.BlockSpec((block, SLOTS * seg_dev), lambda r: (r, 0)), pl.BlockSpec(TOKEN.shape, lambda r: (0, 0))),
        scratch_shapes=[pltpu.VMEM((SLOTS * rows_dev, block, block), jnp.float32)],
        compiler_params=limit(24),
        cost_estimate=pl.CostEstimate(flops=0, bytes_accessed=0, transcendentals=0),
        name="dense_blocks",
    )(block_cols, slot_of, in_hbm(inductance), in_hbm(outgoing))


    sizes = chunk_sizes(width)
    starts = [sum(sizes[:k]) for k in range(len(sizes))]
    whole, *currents = pl.pallas_call(
        inject_kernel,
        out_shape=[
            jax.ShapeDtypeStruct((seg_dev, wide), jnp.bfloat16) for wide in [width] + sizes
        ],
        in_specs=[VMEM, VMEM, ANY],
        out_specs=[VMEM] * (1 + len(sizes)),
        compiler_params=limit(24),
        name="inject_terms",
    )(base_currents, arrived, dense_token)

    def cost():
        return pl.CostEstimate(flops=0, bytes_accessed=0, transcendentals=0)

    beside = send(whole, partner)
    peers = [send(current, across) for current in currents]

    passed = [send(peer, relay) for peer in peers]

    half = 2
    out_type = pltpu.HBM((seg_dev, width), jnp.bfloat16)

    def flux(chunks, others, out, after=()):
        given = [dense, whole, beside] + peers[chunks] + passed[chunks] + others + out
        wide, many = sum(sizes[chunks]), len(sizes[chunks])
        start = starts[chunks][0]
        loose = [item for item in others if start]
        return pl.pallas_call(
            functools.partial(flux_kernel, start, many, True),
            out_shape=(out_type, TOKEN),
            in_specs=[SMEM]
            + [VMEM if start and item is dense else ANY if any(item is other for other in loose) else HBM for item in given]
            + [ANY] * len(after),
            out_specs=(HBM, VMEM),
            scratch_shapes=[
                pltpu.VMEM((1, 8, LANES) if start else (SLOTS, seg_dev, seg_dev), jnp.bfloat16),
                pltpu.VMEM((SLOTS, seg_dev, wide), jnp.bfloat16),
                pltpu.VMEM((seg_dev, wide), jnp.float32),
                pltpu.VMEM((seg_dev, wide), jnp.bfloat16),
                pltpu.SemaphoreType.DMA((SLOTS,)),
                pltpu.SemaphoreType.DMA((SLOTS, many)),
                pltpu.SemaphoreType.DMA,
            ],
            input_output_aliases={len(given): 0} if out else {},
            compiler_params=limit(20 if start else 36),
            cost_estimate=cost(),
            name="flux",
        )(
            flag,
            *[item if any(item is other for other in loose + [dense] * (start > 0)) else in_hbm(item) for item in given],
            *after,
        )

    across_beside = [send(peer, partner) for peer in peers]
    passed_beside = [send(item, partner) for item in passed[:-1]]
    sign = passed[SIGN][:16, :LANES]
    for _ in range(3):
        sign = gate(sign, flag)
    after = [sign]
    others = across_beside[:half] + passed_beside[:half]
    out, token = flux(slice(0, half), others, [], after)
    passed[-1] = gate(passed[-1], token)
    passed_beside.append(send(passed[-1], partner))
    others = across_beside[half:] + passed_beside[half:]
    out, _ = flux(slice(half, len(sizes)), others, [out])
    return out


def solution(mesh):
    placed = (
        P(("group", "row"), None),
        P(("group", "row"), None),
        P(("group", "row"), None),
        P(("group", "row"), None),
        P("row", None, None, None),
        P("row", None),
    )
    return jax.shard_map(
        shards, mesh=mesh, in_specs=placed, out_specs=P(("group", "row"), None), check_vma=False
    )
```

```python
import functools

import jax
import jax.numpy as jnp
from jax import lax
from jax.experimental import pallas as pl
from jax.experimental.pallas import tpu as pltpu
from jax.sharding import PartitionSpec as P

HALO = 2
PIECES = 1
AHEAD = 3
LANES = 128
RADIX = 32
VMEM = pl.BlockSpec(memory_space=pltpu.VMEM)
SMEM = pl.BlockSpec(memory_space=pltpu.SMEM)
HBM = pl.BlockSpec(memory_space=pltpu.HBM)
ANY = pl.BlockSpec(memory_space=pl.ANY)
SLOTS = 2 * HALO + 1
TOKEN = jax.ShapeDtypeStruct((8, LANES), jnp.float32)
WAIT = ('y3', 'z2')
GATE = True
MIB = 1024 * 1024


def limit(mib):
    return pltpu.CompilerParams(vmem_limit_bytes=mib * MIB)


def in_hbm(value):
    return pltpu.with_memory_space_constraint(value, pltpu.HBM)


def gate_kernel(*refs):
    pass


def gate(value, *others):
    return pl.pallas_call(
        gate_kernel,
        out_shape=jax.ShapeDtypeStruct(value.shape, value.dtype),
        in_specs=[ANY] * (1 + len(others)),
        out_specs=ANY,
        input_output_aliases={0: 0},
        compiler_params=limit(1),
        name="gate",
    )(value, *others)


def chunk_sizes(width):
    unit = width // 8
    return [2 * unit, 2 * unit, 2 * unit, 2 * unit]


def pack_kernel(capacity, owner_hbm, target_hbm, rows_hbm, out_ref, owner_ref, target_ref, rows_ref, sems):
    copies = [
        pltpu.make_async_copy(source, target, sems.at[i])
        for i, (source, target) in enumerate(
            [(owner_hbm, owner_ref), (target_hbm, target_ref), (rows_hbm, rows_ref)]
        )
    ]
    for copy in copies:
        copy.start()
    count, width = rows_ref.shape
    slots = out_ref.shape[0]
    tri = lax.broadcasted_iota(jnp.int32, (count, count), 0) < lax.broadcasted_iota(
        jnp.int32, (count, count), 1
    )
    line = lax.broadcasted_iota(jnp.int32, (LANES, count), 0)
    copies[0].wait()
    copies[1].wait()
    owner = owner_ref[...]
    target = target_ref[...]
    named = line == owner
    earlier = jnp.dot(
        named.astype(jnp.bfloat16), tri.astype(jnp.bfloat16), preferred_element_type=jnp.float32
    )
    order = jnp.sum(jnp.where(named, earlier, 0.0), axis=0, keepdims=True).astype(jnp.int32)
    position = owner * capacity + order
    picker = (lax.broadcasted_iota(jnp.int32, (slots, count), 0) == position).astype(jnp.bfloat16)
    tags = jnp.where(line == 0, target // RADIX + 1, jnp.where(line == 1, target % RADIX, 0))
    tags = tags.astype(jnp.float32).astype(jnp.bfloat16)
    out_ref[:, width:] = lax.dot_general(
        picker, tags, (((1,), (1,)), ((), ())), preferred_element_type=jnp.float32
    ).astype(jnp.bfloat16)
    copies[2].wait()
    out_ref[:, :width] = jnp.dot(
        picker, rows_ref[...], preferred_element_type=jnp.float32
    ).astype(jnp.bfloat16)


def inject_kernel(base_ref, arrived_ref, wait_ref, whole_ref, *out_refs):
    offset = 0
    seg_dev = base_ref.shape[0]
    slots = arrived_ref.shape[0]
    width = arrived_ref.shape[1] - LANES
    pick_lane = lax.broadcasted_iota(jnp.int32, (8, LANES), 1)
    weights = jnp.where(pick_lane == 0, float(RADIX), jnp.where(pick_lane == 1, 1.0, 0.0))
    segment = lax.dot_general(
        weights.astype(jnp.bfloat16),
        arrived_ref[:, width:],
        (((1,), (1,)), ((), ())),
        preferred_element_type=jnp.float32,
    )[0:1].astype(jnp.int32) - RADIX
    landing = (lax.broadcasted_iota(jnp.int32, (seg_dev, slots), 0) == segment).astype(jnp.bfloat16)
    for out_ref in out_refs:
        there = slice(offset, offset + out_ref.shape[1])
        injected = jnp.dot(landing, arrived_ref[:, there], preferred_element_type=jnp.float32)
        current = (base_ref[:, there].astype(jnp.float32) + injected).astype(jnp.bfloat16)
        out_ref[...] = current
        whole_ref[:, there] = current
        offset += out_ref.shape[1]


def dense_kernel(cols_ref, slot_ref, blocks_ref, wait_ref, out_ref, token_ref, total_ref):
    row = pl.program_id(0)
    count = blocks_ref.shape[1]
    block = blocks_ref.shape[2]
    per_dev = cols_ref.shape[0]
    places = total_ref.shape[0]
    total_ref[...] = jnp.zeros_like(total_ref)
    token_ref[...] = jnp.zeros_like(token_ref)

    def add(k, carry):
        local = cols_ref[row, k] - slot_ref[SLOTS]
        at = slot_ref[local // per_dev] * per_dev + local % per_dev
        total_ref[at] = total_ref[at] + blocks_ref[0, k].astype(jnp.float32)
        return carry

    lax.fori_loop(0, count, add, 0)
    for at in range(places):
        out_ref[:, at * block : (at + 1) * block] = total_ref[at].astype(jnp.bfloat16)


def hand_kernel(count, flag_ref, *refs):
    peers, passed = refs[:count], refs[count : 2 * count]
    out_refs, sems = refs[-1 - count * PIECES : -1], refs[-1]

    def copies(sources):
        made = []
        for i, out_ref in enumerate(out_refs):
            size = out_ref.shape[1]
            source = sources[i // PIECES].at[:, pl.ds(i % PIECES * size, size)]
            made.append(pltpu.make_async_copy(source, out_ref, sems.at[i]))
        return made

    @pl.when(flag_ref[1] == 0)
    def _():
        for copy in copies(peers):
            copy.start()

    @pl.when(flag_ref[1] == 1)
    def _():
        for copy in copies(passed):
            copy.start()

    for copy in copies(peers):
        copy.wait()


class Slots:
    def __init__(self, flag, dense_ref, slots, matrix, window, mat_sems, sems, first=0):
        self.first = first
        self.flag, self.dense, self.slots = flag, dense_ref, slots
        self.matrix, self.window, self.mat_sems, self.sems = matrix, window, mat_sems, sems

    def block(self, slot):
        depth = self.dense.shape[0]
        if self.matrix is None:
            slot += self.first
            return self.dense[:, slot * depth : (slot + 1) * depth]
        self.columns(slot).wait()
        return self.matrix[slot]

    def columns(self, slot):
        depth = self.dense.shape[0]
        there = self.dense.at[:, pl.ds(slot * depth, depth)]
        return pltpu.make_async_copy(there, self.matrix.at[slot], self.mat_sems.at[slot])

    def rows(self, slot, i, piece):
        before = [item[0] if isinstance(item, tuple) else item for item in self.slots[slot][:i]]
        start = sum(item.shape[1] for item in before)
        target = self.window.at[slot, :, pl.ds(start, piece.shape[1])]
        return pltpu.make_async_copy(piece, target, self.sems.at[slot, i])

    def begin(self, slot):
        if self.matrix is not None:
            self.columns(slot).start()
        for i, piece in enumerate(self.slots[slot]):
            if not isinstance(piece, tuple):
                self.rows(slot, i, piece).start()
                continue
            for value in range(2):
                @pl.when(self.flag == value)
                def _(value=value):
                    self.rows(slot, i, piece[value]).start()

    def sum_into(self, total_ref, prior=None):
        last = len(self.slots) - 1
        for slot in range(min(AHEAD, last + 1)):
            self.begin(slot)
        for slot, pieces in enumerate(self.slots):
            for i, piece in enumerate(pieces):
                self.rows(slot, i, piece[0] if isinstance(piece, tuple) else piece).wait()
            if slot + AHEAD <= last:
                self.begin(slot + AHEAD)
            part = jnp.dot(self.block(slot), self.window[slot], preferred_element_type=jnp.float32)
            if slot == 0 and prior is not None:
                prior.wait()
                total_ref[...] += part
            elif slot == 0:
                total_ref[...] = part
            elif slot < last:
                total_ref[...] += part
        return total_ref[...] + part


def near_kernel(offset, dense_ref, own, beside, wait_ref, total_ref, token_ref, window, sems):
    token_ref[...] = jnp.zeros_like(token_ref)
    there = pl.ds(offset, total_ref.shape[1])
    slots = [[own.at[:, there]], [beside.at[:, there]]]
    total_ref[...] = Slots(0, dense_ref, slots, None, window, None, sems).sum_into(total_ref)


def flux_kernel(offset, count, flag_ref, dense_ref, own, beside, *refs):
    out_ref, token_ref, matrix, window, total, result, mat_sems, sems, out_sem = refs[-9:]
    token_ref[...] = jnp.zeros_like(token_ref)
    there = pl.ds(offset, total.shape[1])
    peers, passed = refs[:count], refs[count : 2 * count]
    pairs = list(zip(refs[2 * count : 3 * count], refs[3 * count : 4 * count]))
    slots = [[own.at[:, there]], [beside.at[:, there]], peers, passed, pairs]
    parts = Slots(flag_ref[0], dense_ref, slots, matrix, window, mat_sems, sems).sum_into(total)
    result[...] = parts.astype(jnp.bfloat16)
    out = pltpu.make_async_copy(result, out_ref.at[:, there], out_sem)
    out.start()
    out.wait()


def far_kernel(offset, count, flag_ref, dense_ref, prior_ref, *refs):
    out_ref, window, total, result, sems, prior_sem, out_sem = refs[-7:]
    there = pl.ds(offset, total.shape[1])
    prior = pltpu.make_async_copy(prior_ref, total, prior_sem)
    peers, passed = refs[:count], refs[count : 2 * count]
    pairs = list(zip(refs[2 * count : 3 * count], refs[3 * count : 4 * count]))
    slots = Slots(flag_ref[0], dense_ref, [peers, passed, pairs], None, window, None, sems, first=2)
    prior.start()
    result[...] = slots.sum_into(total, prior).astype(jnp.bfloat16)
    out = pltpu.make_async_copy(result, out_ref.at[:, there], out_sem)
    out.start()
    out.wait()


def shards(base_currents, term_rows, term_owner, term_slot, inductance, block_cols):
    devices = lax.axis_size("row")
    me = lax.axis_index("row")
    seg_dev, width = base_currents.shape
    capacity = max(2, 2 * term_rows.shape[0] // devices)
    slots = devices * capacity
    rows_dev, count, block, _ = inductance.shape

    core, side = me % 2, (me // 2) % 2
    across = [(i, i ^ 2) for i in range(devices)]
    partner = [(i, i ^ 1) for i in range(devices)]
    relay = [(i, (i - 4 if i & 2 else i + 4) % devices) for i in range(devices)]

    def send(value, pairs):
        return lax.ppermute(value, "row", pairs)

    near = jnp.where(core == 0, 4, 1)
    far = jnp.where(core == 0, 1, 4)
    slot_of = jnp.stack(
        [
            jnp.where(side == 0, 3, 2),
            near,
            jnp.zeros_like(near),
            far,
            jnp.where(side == 0, 2, 3),
            (me - HALO) * rows_dev,
        ]
    ).astype(jnp.int32)
    flag = jnp.stack([core == side, core != side]).astype(jnp.int32)

    outgoing = pl.pallas_call(
        functools.partial(pack_kernel, capacity),
        out_shape=jax.ShapeDtypeStruct((slots, width + LANES), jnp.bfloat16),
        in_specs=[HBM] * 3,
        out_specs=VMEM,
        scratch_shapes=[
            pltpu.VMEM((1, term_rows.shape[0]), jnp.int32),
            pltpu.VMEM((1, term_rows.shape[0]), jnp.int32),
            pltpu.VMEM(term_rows.shape, jnp.bfloat16),
            pltpu.SemaphoreType.DMA((3,)),
        ],
        compiler_params=limit(16),
        name="pack_terms",
    )(*[in_hbm(item) for item in (term_owner.reshape(1, -1), term_slot.reshape(1, -1), term_rows)])
    arrived = lax.all_to_all(
        outgoing.reshape(devices, capacity, width + LANES), "row", split_axis=0, concat_axis=0, tiled=True
    ).reshape(slots, width + LANES)

    dense, dense_token = pl.pallas_call(
        dense_kernel,
        out_shape=(pltpu.HBM((seg_dev, SLOTS * seg_dev), jnp.bfloat16), TOKEN),
        grid=(rows_dev,),
        in_specs=[SMEM, SMEM, pl.BlockSpec((1, count, block, block), lambda r: (r, 0, 0, 0)), HBM],
        out_specs=(pl.BlockSpec((block, SLOTS * seg_dev), lambda r: (r, 0)), pl.BlockSpec(TOKEN.shape, lambda r: (0, 0))),
        scratch_shapes=[pltpu.VMEM((SLOTS * rows_dev, block, block), jnp.float32)],
        compiler_params=limit(24),
        cost_estimate=pl.CostEstimate(flops=0, bytes_accessed=0, transcendentals=0),
        name="dense_blocks",
    )(block_cols, slot_of, in_hbm(inductance), in_hbm(outgoing))


    sizes = chunk_sizes(width)
    starts = [sum(sizes[:k]) for k in range(len(sizes))]
    whole, *currents = pl.pallas_call(
        inject_kernel,
        out_shape=[
            jax.ShapeDtypeStruct((seg_dev, wide), jnp.bfloat16) for wide in [width] + sizes
        ],
        in_specs=[VMEM, VMEM, ANY],
        out_specs=[VMEM] * (1 + len(sizes)),
        compiler_params=limit(24),
        name="inject_terms",
    )(base_currents, arrived, dense_token)

    def cost():
        return pl.CostEstimate(flops=0, bytes_accessed=0, transcendentals=0)

    beside = send(whole, partner)
    peers = [send(current, across) for current in currents]

    passed = [send(peer, relay) for peer in peers]

    half = 2
    out_type = pltpu.HBM((seg_dev, width), jnp.bfloat16)

    across_beside = [send(peer, partner) for peer in peers]
    passed_beside = [send(item, partner) for item in passed[:-1]]
    sign = passed[half][:16, :LANES]
    for _ in range(3):
        sign = gate(sign, flag)

    wide = sum(sizes[:half])
    given = [dense, whole, beside] + peers[:half] + passed[:half]
    given += across_beside[:half] + passed_beside[:half]
    out, token = pl.pallas_call(
        functools.partial(flux_kernel, 0, half),
        out_shape=(out_type, TOKEN),
        in_specs=[SMEM] + [HBM] * len(given) + [ANY],
        out_specs=(HBM, VMEM),
        scratch_shapes=[
            pltpu.VMEM((SLOTS, seg_dev, seg_dev), jnp.bfloat16),
            pltpu.VMEM((SLOTS, seg_dev, wide), jnp.bfloat16),
            pltpu.VMEM((seg_dev, wide), jnp.float32),
            pltpu.VMEM((seg_dev, wide), jnp.bfloat16),
            pltpu.SemaphoreType.DMA((SLOTS,)),
            pltpu.SemaphoreType.DMA((SLOTS, half)),
            pltpu.SemaphoreType.DMA,
        ],
        compiler_params=limit(36),
        cost_estimate=cost(),
        name="flux",
    )(flag, *[in_hbm(item) for item in given], sign)

    rest, left = width - wide, len(sizes) - half
    sums, token = pl.pallas_call(
        functools.partial(near_kernel, wide),
        out_shape=(jax.ShapeDtypeStruct((seg_dev, rest), jnp.float32), TOKEN),
        in_specs=[VMEM, HBM, HBM, ANY],
        out_specs=(VMEM, VMEM),
        scratch_shapes=[
            pltpu.VMEM((2, seg_dev, rest), jnp.bfloat16),
            pltpu.SemaphoreType.DMA((2, 1)),
        ],
        compiler_params=limit(16),
        cost_estimate=cost(),
        name="near_flux",
    )(dense, in_hbm(whole), in_hbm(beside), token)
    passed[-1] = gate(passed[-1], token)
    passed_beside.append(send(passed[-1], partner))
    given = peers[half:] + passed[half:] + across_beside[half:] + passed_beside[half:]
    return pl.pallas_call(
        functools.partial(far_kernel, wide, left),
        out_shape=out_type,
        in_specs=[SMEM, VMEM] + [ANY] * (1 + len(given)) + [HBM],
        out_specs=HBM,
        scratch_shapes=[
            pltpu.VMEM((3, seg_dev, rest), jnp.bfloat16),
            pltpu.VMEM((seg_dev, rest), jnp.float32),
            pltpu.VMEM((seg_dev, rest), jnp.bfloat16),
            pltpu.SemaphoreType.DMA((3, left)),
            pltpu.SemaphoreType.DMA,
            pltpu.SemaphoreType.DMA,
        ],
        input_output_aliases={3 + len(given): 0},
        compiler_params=limit(16),
        cost_estimate=cost(),
        name="far_flux",
    )(flag, dense, sums, *given, in_hbm(out))


def solution(mesh):
    placed = (
        P(("group", "row"), None),
        P(("group", "row"), None),
        P(("group", "row"), None),
        P(("group", "row"), None),
        P("row", None, None, None),
        P("row", None),
    )
    return jax.shard_map(
        shards, mesh=mesh, in_specs=placed, out_specs=P(("group", "row"), None), check_vma=False
    )
```

```python
import functools

import jax
import jax.numpy as jnp
from jax import lax
from jax.experimental import pallas as pl
from jax.experimental.pallas import tpu as pltpu
from jax.sharding import PartitionSpec as P

HALO = 2
PIECES = 1
AHEAD = 3
LANES = 128
RADIX = 32
VMEM = pl.BlockSpec(memory_space=pltpu.VMEM)
SMEM = pl.BlockSpec(memory_space=pltpu.SMEM)
HBM = pl.BlockSpec(memory_space=pltpu.HBM)
ANY = pl.BlockSpec(memory_space=pl.ANY)
SLOTS = 2 * HALO + 1
TOKEN = jax.ShapeDtypeStruct((8, LANES), jnp.float32)
WAIT = ('y3', 'z2')
GATE = True
MIB = 1024 * 1024


def limit(mib):
    return pltpu.CompilerParams(vmem_limit_bytes=mib * MIB)


def in_hbm(value):
    return pltpu.with_memory_space_constraint(value, pltpu.HBM)


def gate_kernel(*refs):
    pass


def gate(value, *others):
    return pl.pallas_call(
        gate_kernel,
        out_shape=jax.ShapeDtypeStruct(value.shape, value.dtype),
        in_specs=[ANY] * (1 + len(others)),
        out_specs=ANY,
        input_output_aliases={0: 0},
        compiler_params=limit(1),
        name="gate",
    )(value, *others)


def chunk_sizes(width):
    unit = width // 8
    return [2 * unit, 2 * unit, 2 * unit, 2 * unit]


def pack_kernel(capacity, owner_hbm, target_hbm, rows_hbm, out_hbm, owner_ref, target_ref, rows_ref, out_ref, sems, out_sems):
    copies = [
        pltpu.make_async_copy(source, target, sems.at[i])
        for i, (source, target) in enumerate(
            [(owner_hbm, owner_ref), (target_hbm, target_ref), (rows_hbm, rows_ref)]
        )
    ]
    for copy in copies:
        copy.start()
    count, width = rows_ref.shape
    slots = out_ref.shape[0]
    tri = lax.broadcasted_iota(jnp.int32, (count, count), 0) < lax.broadcasted_iota(
        jnp.int32, (count, count), 1
    )
    line = lax.broadcasted_iota(jnp.int32, (LANES, count), 0)
    copies[0].wait()
    copies[1].wait()
    owner = owner_ref[...]
    target = target_ref[...]
    named = line == owner
    earlier = jnp.dot(
        named.astype(jnp.bfloat16), tri.astype(jnp.bfloat16), preferred_element_type=jnp.float32
    )
    order = jnp.sum(jnp.where(named, earlier, 0.0), axis=0, keepdims=True).astype(jnp.int32)
    position = owner * capacity + order
    picker = (lax.broadcasted_iota(jnp.int32, (slots, count), 0) == position).astype(jnp.bfloat16)
    tags = jnp.where(line == 0, target // RADIX + 1, jnp.where(line == 1, target % RADIX, 0))
    tags = tags.astype(jnp.float32).astype(jnp.bfloat16)
    out_ref[:, width:] = lax.dot_general(
        picker, tags, (((1,), (1,)), ((), ())), preferred_element_type=jnp.float32
    ).astype(jnp.bfloat16)
    ends = [pl.ds(width, LANES), pl.ds(0, width // 2), pl.ds(width // 2, width // 2)]
    outs = [
        pltpu.make_async_copy(out_ref.at[:, end], out_hbm.at[:, end], out_sems.at[i])
        for i, end in enumerate(ends)
    ]
    outs[0].start()
    copies[2].wait()
    for end, out in zip(ends[1:], outs[1:]):
        out_ref[:, end] = jnp.dot(
            picker, rows_ref[:, end], preferred_element_type=jnp.float32
        ).astype(jnp.bfloat16)
        out.start()
    for out in outs:
        out.wait()


def inject_kernel(base_ref, arrived_ref, wait_ref, whole_ref, *out_refs):
    offset = 0
    seg_dev = base_ref.shape[0]
    slots = arrived_ref.shape[0]
    width = arrived_ref.shape[1] - LANES
    pick_lane = lax.broadcasted_iota(jnp.int32, (8, LANES), 1)
    weights = jnp.where(pick_lane == 0, float(RADIX), jnp.where(pick_lane == 1, 1.0, 0.0))
    segment = lax.dot_general(
        weights.astype(jnp.bfloat16),
        arrived_ref[:, width:],
        (((1,), (1,)), ((), ())),
        preferred_element_type=jnp.float32,
    )[0:1].astype(jnp.int32) - RADIX
    landing = (lax.broadcasted_iota(jnp.int32, (seg_dev, slots), 0) == segment).astype(jnp.bfloat16)
    for out_ref in out_refs:
        there = slice(offset, offset + out_ref.shape[1])
        injected = jnp.dot(landing, arrived_ref[:, there], preferred_element_type=jnp.float32)
        current = (base_ref[:, there].astype(jnp.float32) + injected).astype(jnp.bfloat16)
        out_ref[...] = current
        whole_ref[:, there] = current
        offset += out_ref.shape[1]


def dense_kernel(cols_ref, slot_ref, blocks_ref, wait_ref, out_ref, token_ref, total_ref):
    row = pl.program_id(0)
    count = blocks_ref.shape[1]
    block = blocks_ref.shape[2]
    per_dev = cols_ref.shape[0]
    places = total_ref.shape[0]
    total_ref[...] = jnp.zeros_like(total_ref)
    token_ref[...] = jnp.zeros_like(token_ref)

    def add(k, carry):
        local = cols_ref[row, k] - slot_ref[SLOTS]
        at = slot_ref[local // per_dev] * per_dev + local % per_dev
        total_ref[at] = total_ref[at] + blocks_ref[0, k].astype(jnp.float32)
        return carry

    lax.fori_loop(0, count, add, 0)
    for at in range(places):
        out_ref[:, at * block : (at + 1) * block] = total_ref[at].astype(jnp.bfloat16)


def hand_kernel(count, flag_ref, *refs):
    peers, passed = refs[:count], refs[count : 2 * count]
    out_refs, sems = refs[-1 - count * PIECES : -1], refs[-1]

    def copies(sources):
        made = []
        for i, out_ref in enumerate(out_refs):
            size = out_ref.shape[1]
            source = sources[i // PIECES].at[:, pl.ds(i % PIECES * size, size)]
            made.append(pltpu.make_async_copy(source, out_ref, sems.at[i]))
        return made

    @pl.when(flag_ref[1] == 0)
    def _():
        for copy in copies(peers):
            copy.start()

    @pl.when(flag_ref[1] == 1)
    def _():
        for copy in copies(passed):
            copy.start()

    for copy in copies(peers):
        copy.wait()


class Slots:
    def __init__(self, flag, dense_ref, slots, matrix, window, mat_sems, sems, first=0):
        self.first = first
        self.flag, self.dense, self.slots = flag, dense_ref, slots
        self.matrix, self.window, self.mat_sems, self.sems = matrix, window, mat_sems, sems

    def block(self, slot):
        depth = self.dense.shape[0]
        if self.matrix is None:
            slot += self.first
            return self.dense[:, slot * depth : (slot + 1) * depth]
        self.columns(slot).wait()
        return self.matrix[slot]

    def columns(self, slot):
        depth = self.dense.shape[0]
        there = self.dense.at[:, pl.ds(slot * depth, depth)]
        return pltpu.make_async_copy(there, self.matrix.at[slot], self.mat_sems.at[slot])

    def rows(self, slot, i, piece):
        before = [item[0] if isinstance(item, tuple) else item for item in self.slots[slot][:i]]
        start = sum(item.shape[1] for item in before)
        target = self.window.at[slot, :, pl.ds(start, piece.shape[1])]
        return pltpu.make_async_copy(piece, target, self.sems.at[slot, i])

    def begin(self, slot):
        if self.matrix is not None:
            self.columns(slot).start()
        for i, piece in enumerate(self.slots[slot]):
            if not isinstance(piece, tuple):
                self.rows(slot, i, piece).start()
                continue
            for value in range(2):
                @pl.when(self.flag == value)
                def _(value=value):
                    self.rows(slot, i, piece[value]).start()

    def sum_into(self, total_ref, prior=None):
        last = len(self.slots) - 1
        for slot in range(min(AHEAD, last + 1)):
            self.begin(slot)
        for slot, pieces in enumerate(self.slots):
            for i, piece in enumerate(pieces):
                self.rows(slot, i, piece[0] if isinstance(piece, tuple) else piece).wait()
            if slot + AHEAD <= last:
                self.begin(slot + AHEAD)
            part = jnp.dot(self.block(slot), self.window[slot], preferred_element_type=jnp.float32)
            if slot == 0 and prior is not None:
                prior.wait()
                total_ref[...] += part
            elif slot == 0:
                total_ref[...] = part
            elif slot < last:
                total_ref[...] += part
        return total_ref[...] + part


def near_kernel(offset, dense_ref, own, beside, wait_ref, total_ref, token_ref, window, sems):
    token_ref[...] = jnp.zeros_like(token_ref)
    there = pl.ds(offset, total_ref.shape[1])
    slots = [[own.at[:, there]], [beside.at[:, there]]]
    total_ref[...] = Slots(0, dense_ref, slots, None, window, None, sems).sum_into(total_ref)


def flux_kernel(offset, count, flag_ref, dense_ref, own, beside, *refs):
    out_ref, token_ref, matrix, window, total, result, mat_sems, sems, out_sem = refs[-9:]
    token_ref[...] = jnp.zeros_like(token_ref)
    there = pl.ds(offset, total.shape[1])
    peers, passed = refs[:count], refs[count : 2 * count]
    pairs = list(zip(refs[2 * count : 3 * count], refs[3 * count : 4 * count]))
    slots = [[own.at[:, there]], [beside.at[:, there]], peers, passed, pairs]
    parts = Slots(flag_ref[0], dense_ref, slots, matrix, window, mat_sems, sems).sum_into(total)
    result[...] = parts.astype(jnp.bfloat16)
    out = pltpu.make_async_copy(result, out_ref.at[:, there], out_sem)
    out.start()
    out.wait()


def far_kernel(offset, count, flag_ref, dense_ref, prior_ref, *refs):
    out_ref, window, total, result, sems, prior_sem, out_sem = refs[-7:]
    there = pl.ds(offset, total.shape[1])
    prior = pltpu.make_async_copy(prior_ref, total, prior_sem)
    peers, passed = refs[:count], refs[count : 2 * count]
    pairs = list(zip(refs[2 * count : 3 * count], refs[3 * count : 4 * count]))
    slots = Slots(flag_ref[0], dense_ref, [peers, passed, pairs], None, window, None, sems, first=2)
    prior.start()
    result[...] = slots.sum_into(total, prior).astype(jnp.bfloat16)
    out = pltpu.make_async_copy(result, out_ref.at[:, there], out_sem)
    out.start()
    out.wait()


def shards(base_currents, term_rows, term_owner, term_slot, inductance, block_cols):
    devices = lax.axis_size("row")
    me = lax.axis_index("row")
    seg_dev, width = base_currents.shape
    capacity = max(2, 2 * term_rows.shape[0] // devices)
    slots = devices * capacity
    rows_dev, count, block, _ = inductance.shape

    core, side = me % 2, (me // 2) % 2
    across = [(i, i ^ 2) for i in range(devices)]
    partner = [(i, i ^ 1) for i in range(devices)]
    relay = [(i, (i - 4 if i & 2 else i + 4) % devices) for i in range(devices)]

    def send(value, pairs):
        return lax.ppermute(value, "row", pairs)

    near = jnp.where(core == 0, 4, 1)
    far = jnp.where(core == 0, 1, 4)
    slot_of = jnp.stack(
        [
            jnp.where(side == 0, 3, 2),
            near,
            jnp.zeros_like(near),
            far,
            jnp.where(side == 0, 2, 3),
            (me - HALO) * rows_dev,
        ]
    ).astype(jnp.int32)
    flag = jnp.stack([core == side, core != side]).astype(jnp.int32)

    outgoing = pl.pallas_call(
        functools.partial(pack_kernel, capacity),
        out_shape=pltpu.HBM((slots, width + LANES), jnp.bfloat16),
        in_specs=[HBM] * 3,
        out_specs=HBM,
        scratch_shapes=[
            pltpu.VMEM((1, term_rows.shape[0]), jnp.int32),
            pltpu.VMEM((1, term_rows.shape[0]), jnp.int32),
            pltpu.VMEM(term_rows.shape, jnp.bfloat16),
            pltpu.VMEM((slots, width + LANES), jnp.bfloat16),
            pltpu.SemaphoreType.DMA((3,)),
            pltpu.SemaphoreType.DMA((3,)),
        ],
        compiler_params=limit(16),
        name="pack_terms",
    )(*[in_hbm(item) for item in (term_owner.reshape(1, -1), term_slot.reshape(1, -1), term_rows)])
    arrived = lax.all_to_all(
        outgoing.reshape(devices, capacity, width + LANES), "row", split_axis=0, concat_axis=0, tiled=True
    ).reshape(slots, width + LANES)

    dense, dense_token = pl.pallas_call(
        dense_kernel,
        out_shape=(pltpu.HBM((seg_dev, SLOTS * seg_dev), jnp.bfloat16), TOKEN),
        grid=(rows_dev,),
        in_specs=[SMEM, SMEM, pl.BlockSpec((1, count, block, block), lambda r: (r, 0, 0, 0)), HBM],
        out_specs=(pl.BlockSpec((block, SLOTS * seg_dev), lambda r: (r, 0)), pl.BlockSpec(TOKEN.shape, lambda r: (0, 0))),
        scratch_shapes=[pltpu.VMEM((SLOTS * rows_dev, block, block), jnp.float32)],
        compiler_params=limit(24),
        cost_estimate=pl.CostEstimate(flops=0, bytes_accessed=0, transcendentals=0),
        name="dense_blocks",
    )(block_cols, slot_of, in_hbm(inductance), in_hbm(outgoing))


    sizes = chunk_sizes(width)
    starts = [sum(sizes[:k]) for k in range(len(sizes))]
    whole, *currents = pl.pallas_call(
        inject_kernel,
        out_shape=[
            jax.ShapeDtypeStruct((seg_dev, wide), jnp.bfloat16) for wide in [width] + sizes
        ],
        in_specs=[VMEM, VMEM, ANY],
        out_specs=[VMEM] * (1 + len(sizes)),
        compiler_params=limit(24),
        name="inject_terms",
    )(base_currents, arrived, dense_token)

    def cost():
        return pl.CostEstimate(flops=0, bytes_accessed=0, transcendentals=0)

    beside = send(whole, partner)
    peers = [send(current, across) for current in currents]

    passed = [send(peer, relay) for peer in peers]

    half = 2
    out_type = pltpu.HBM((seg_dev, width), jnp.bfloat16)

    across_beside = [send(peer, partner) for peer in peers]
    passed_beside = [send(item, partner) for item in passed[:-1]]
    sign = passed[half][:16, :LANES]
    for _ in range(3):
        sign = gate(sign, flag)

    wide = sum(sizes[:half])
    given = [dense, whole, beside] + peers[:half] + passed[:half]
    given += across_beside[:half] + passed_beside[:half]
    out, token = pl.pallas_call(
        functools.partial(flux_kernel, 0, half),
        out_shape=(out_type, TOKEN),
        in_specs=[SMEM] + [HBM] * len(given) + [ANY],
        out_specs=(HBM, VMEM),
        scratch_shapes=[
            pltpu.VMEM((SLOTS, seg_dev, seg_dev), jnp.bfloat16),
            pltpu.VMEM((SLOTS, seg_dev, wide), jnp.bfloat16),
            pltpu.VMEM((seg_dev, wide), jnp.float32),
            pltpu.VMEM((seg_dev, wide), jnp.bfloat16),
            pltpu.SemaphoreType.DMA((SLOTS,)),
            pltpu.SemaphoreType.DMA((SLOTS, half)),
            pltpu.SemaphoreType.DMA,
        ],
        compiler_params=limit(36),
        cost_estimate=cost(),
        name="flux",
    )(flag, *[in_hbm(item) for item in given], sign)

    rest, left = width - wide, len(sizes) - half
    sums, token = pl.pallas_call(
        functools.partial(near_kernel, wide),
        out_shape=(jax.ShapeDtypeStruct((seg_dev, rest), jnp.float32), TOKEN),
        in_specs=[VMEM, HBM, HBM, ANY],
        out_specs=(VMEM, VMEM),
        scratch_shapes=[
            pltpu.VMEM((2, seg_dev, rest), jnp.bfloat16),
            pltpu.SemaphoreType.DMA((2, 1)),
        ],
        compiler_params=limit(16),
        cost_estimate=cost(),
        name="near_flux",
    )(dense, in_hbm(whole), in_hbm(beside), token)
    passed[-1] = gate(passed[-1], token)
    passed_beside.append(send(passed[-1], partner))
    given = peers[half:] + passed[half:] + across_beside[half:] + passed_beside[half:]
    return pl.pallas_call(
        functools.partial(far_kernel, wide, left),
        out_shape=out_type,
        in_specs=[SMEM, VMEM] + [ANY] * (1 + len(given)) + [HBM],
        out_specs=HBM,
        scratch_shapes=[
            pltpu.VMEM((3, seg_dev, rest), jnp.bfloat16),
            pltpu.VMEM((seg_dev, rest), jnp.float32),
            pltpu.VMEM((seg_dev, rest), jnp.bfloat16),
            pltpu.SemaphoreType.DMA((3, left)),
            pltpu.SemaphoreType.DMA,
            pltpu.SemaphoreType.DMA,
        ],
        input_output_aliases={3 + len(given): 0},
        compiler_params=limit(16),
        cost_estimate=cost(),
        name="far_flux",
    )(flag, dense, sums, *given, in_hbm(out))


def solution(mesh):
    placed = (
        P(("group", "row"), None),
        P(("group", "row"), None),
        P(("group", "row"), None),
        P(("group", "row"), None),
        P("row", None, None, None),
        P("row", None),
    )
    return jax.shard_map(
        shards, mesh=mesh, in_specs=placed, out_specs=P(("group", "row"), None), check_vma=False
    )
```

```python
import functools

import jax
import jax.numpy as jnp
from jax import lax
from jax.experimental import pallas as pl
from jax.experimental.pallas import tpu as pltpu
from jax.sharding import PartitionSpec as P

HALO = 2
PIECES = 1
AHEAD = 3
LANES = 128
RADIX = 32
VMEM = pl.BlockSpec(memory_space=pltpu.VMEM)
SMEM = pl.BlockSpec(memory_space=pltpu.SMEM)
HBM = pl.BlockSpec(memory_space=pltpu.HBM)
ANY = pl.BlockSpec(memory_space=pl.ANY)
SLOTS = 2 * HALO + 1
TOKEN = jax.ShapeDtypeStruct((8, LANES), jnp.float32)
WAIT = ('y3', 'z2')
GATE = True
MIB = 1024 * 1024


def limit(mib):
    return pltpu.CompilerParams(vmem_limit_bytes=mib * MIB)


def in_hbm(value):
    return pltpu.with_memory_space_constraint(value, pltpu.HBM)


def gate_kernel(*refs):
    pass


def gate(value, *others):
    return pl.pallas_call(
        gate_kernel,
        out_shape=jax.ShapeDtypeStruct(value.shape, value.dtype),
        in_specs=[ANY] * (1 + len(others)),
        out_specs=ANY,
        input_output_aliases={0: 0},
        compiler_params=limit(1),
        name="gate",
    )(value, *others)


def chunk_sizes(width):
    unit = width // 8
    return [2 * unit, 2 * unit, 2 * unit, 2 * unit]


def pack_kernel(capacity, owner_hbm, target_hbm, rows_hbm, out_hbm, owner_ref, target_ref, rows_ref, out_ref, sems, out_sems):
    copies = [
        pltpu.make_async_copy(source, target, sems.at[i])
        for i, (source, target) in enumerate(
            [(owner_hbm, owner_ref), (target_hbm, target_ref), (rows_hbm, rows_ref)]
        )
    ]
    for copy in copies:
        copy.start()
    count, width = rows_ref.shape
    slots = out_ref.shape[0]
    tri = lax.broadcasted_iota(jnp.int32, (count, count), 0) < lax.broadcasted_iota(
        jnp.int32, (count, count), 1
    )
    line = lax.broadcasted_iota(jnp.int32, (LANES, count), 0)
    copies[0].wait()
    copies[1].wait()
    owner = owner_ref[...]
    target = target_ref[...]
    named = line == owner
    earlier = jnp.dot(
        named.astype(jnp.bfloat16), tri.astype(jnp.bfloat16), preferred_element_type=jnp.float32
    )
    order = jnp.sum(jnp.where(named, earlier, 0.0), axis=0, keepdims=True).astype(jnp.int32)
    position = owner * capacity + order
    picker = (lax.broadcasted_iota(jnp.int32, (slots, count), 0) == position).astype(jnp.bfloat16)
    tags = jnp.where(line == 0, target // RADIX + 1, jnp.where(line == 1, target % RADIX, 0))
    tags = tags.astype(jnp.float32).astype(jnp.bfloat16)
    out_ref[:, width:] = lax.dot_general(
        picker, tags, (((1,), (1,)), ((), ())), preferred_element_type=jnp.float32
    ).astype(jnp.bfloat16)
    ends = [pl.ds(width, LANES), pl.ds(0, width // 2), pl.ds(width // 2, width // 2)]
    outs = [
        pltpu.make_async_copy(out_ref.at[:, end], out_hbm.at[:, end], out_sems.at[i])
        for i, end in enumerate(ends)
    ]
    outs[0].start()
    copies[2].wait()
    for end, out in zip(ends[1:], outs[1:]):
        out_ref[:, end] = jnp.dot(
            picker, rows_ref[:, end], preferred_element_type=jnp.float32
        ).astype(jnp.bfloat16)
        out.start()
    for out in outs:
        out.wait()


def inject_kernel(base_ref, arrived_ref, wait_ref, whole_ref, *out_refs):
    offset = 0
    seg_dev = base_ref.shape[0]
    slots = arrived_ref.shape[0]
    width = arrived_ref.shape[1] - LANES
    pick_lane = lax.broadcasted_iota(jnp.int32, (8, LANES), 1)
    weights = jnp.where(pick_lane == 0, float(RADIX), jnp.where(pick_lane == 1, 1.0, 0.0))
    segment = lax.dot_general(
        weights.astype(jnp.bfloat16),
        arrived_ref[:, width:],
        (((1,), (1,)), ((), ())),
        preferred_element_type=jnp.float32,
    )[0:1].astype(jnp.int32) - RADIX
    landing = (lax.broadcasted_iota(jnp.int32, (seg_dev, slots), 0) == segment).astype(jnp.bfloat16)
    for out_ref in out_refs:
        there = slice(offset, offset + out_ref.shape[1])
        injected = jnp.dot(landing, arrived_ref[:, there], preferred_element_type=jnp.float32)
        current = (base_ref[:, there].astype(jnp.float32) + injected).astype(jnp.bfloat16)
        out_ref[...] = current
        whole_ref[:, there] = current
        offset += out_ref.shape[1]


def dense_kernel(cols_ref, slot_ref, blocks_ref, wait_ref, out_ref, token_ref, total_ref):
    row = pl.program_id(0)
    count = blocks_ref.shape[1]
    block = blocks_ref.shape[2]
    per_dev = cols_ref.shape[0]
    places = total_ref.shape[0]
    total_ref[...] = jnp.zeros_like(total_ref)
    token_ref[...] = jnp.zeros_like(token_ref)

    def add(k, carry):
        local = cols_ref[row, k] - slot_ref[SLOTS]
        at = slot_ref[local // per_dev] * per_dev + local % per_dev
        total_ref[at] = total_ref[at] + blocks_ref[0, k].astype(jnp.float32)
        return carry

    lax.fori_loop(0, count, add, 0)
    for at in range(places):
        out_ref[:, at * block : (at + 1) * block] = total_ref[at].astype(jnp.bfloat16)


def hand_kernel(count, flag_ref, *refs):
    peers, passed = refs[:count], refs[count : 2 * count]
    out_refs, sems = refs[-1 - count * PIECES : -1], refs[-1]

    def copies(sources):
        made = []
        for i, out_ref in enumerate(out_refs):
            size = out_ref.shape[1]
            source = sources[i // PIECES].at[:, pl.ds(i % PIECES * size, size)]
            made.append(pltpu.make_async_copy(source, out_ref, sems.at[i]))
        return made

    @pl.when(flag_ref[1] == 0)
    def _():
        for copy in copies(peers):
            copy.start()

    @pl.when(flag_ref[1] == 1)
    def _():
        for copy in copies(passed):
            copy.start()

    for copy in copies(peers):
        copy.wait()


class Slots:
    def __init__(self, flag, dense_ref, slots, matrix, window, mat_sems, sems, first=0):
        self.first = first
        self.flag, self.dense, self.slots = flag, dense_ref, slots
        self.matrix, self.window, self.mat_sems, self.sems = matrix, window, mat_sems, sems

    def block(self, slot):
        depth = self.dense.shape[0]
        if self.matrix is None:
            slot += self.first
            return self.dense[:, slot * depth : (slot + 1) * depth]
        self.columns(slot).wait()
        return self.matrix[slot]

    def columns(self, slot):
        depth = self.dense.shape[0]
        there = self.dense.at[:, pl.ds(slot * depth, depth)]
        return pltpu.make_async_copy(there, self.matrix.at[slot], self.mat_sems.at[slot])

    def rows(self, slot, i, piece):
        before = [item[0] if isinstance(item, tuple) else item for item in self.slots[slot][:i]]
        start = sum(item.shape[1] for item in before)
        target = self.window.at[slot, :, pl.ds(start, piece.shape[1])]
        return pltpu.make_async_copy(piece, target, self.sems.at[slot, i])

    def begin(self, slot):
        if self.matrix is not None:
            self.columns(slot).start()
        for i, piece in enumerate(self.slots[slot]):
            if not isinstance(piece, tuple):
                self.rows(slot, i, piece).start()
                continue
            for value in range(2):
                @pl.when(self.flag == value)
                def _(value=value):
                    self.rows(slot, i, piece[value]).start()

    def sum_into(self, total_ref, prior=None):
        last = len(self.slots) - 1
        for slot in range(min(AHEAD, last + 1)):
            self.begin(slot)
        for slot, pieces in enumerate(self.slots):
            for i, piece in enumerate(pieces):
                self.rows(slot, i, piece[0] if isinstance(piece, tuple) else piece).wait()
            if slot + AHEAD <= last:
                self.begin(slot + AHEAD)
            part = jnp.dot(self.block(slot), self.window[slot], preferred_element_type=jnp.float32)
            if slot == 0 and prior is not None:
                prior.wait()
                total_ref[...] += part
            elif slot == 0:
                total_ref[...] = part
            elif slot < last:
                total_ref[...] += part
        return total_ref[...] + part


def near_kernel(offset, dense_ref, own, beside, wait_ref, total_ref, token_ref, window, sems):
    token_ref[...] = jnp.zeros_like(token_ref)
    there = pl.ds(offset, total_ref.shape[1])
    slots = [[own.at[:, there]], [beside.at[:, there]]]
    total_ref[...] = Slots(0, dense_ref, slots, None, window, None, sems).sum_into(total_ref)


def flux_kernel(offset, count, flag_ref, dense_ref, own, beside, *refs):
    out_ref, token_ref, matrix, window, total, result, mat_sems, sems, out_sem = refs[-9:]
    token_ref[...] = jnp.zeros_like(token_ref)
    there = pl.ds(offset, total.shape[1])
    peers, passed = refs[:count], refs[count : 2 * count]
    pairs = list(zip(refs[2 * count : 3 * count], refs[3 * count : 4 * count]))
    slots = [[own.at[:, there]], [beside.at[:, there]], peers, passed, pairs]
    parts = Slots(flag_ref[0], dense_ref, slots, matrix, window, mat_sems, sems).sum_into(total)
    result[...] = parts.astype(jnp.bfloat16)
    out = pltpu.make_async_copy(result, out_ref.at[:, there], out_sem)
    out.start()
    out.wait()


def far_kernel(offset, count, flag_ref, dense_ref, prior_ref, *refs):
    out_ref, window, total, result, sems, prior_sem, out_sem = refs[-7:]
    there = pl.ds(offset, total.shape[1])
    prior = pltpu.make_async_copy(prior_ref, total, prior_sem)
    peers, passed = refs[:count], refs[count : 2 * count]
    pairs = list(zip(refs[2 * count : 3 * count], refs[3 * count : 4 * count]))
    slots = Slots(flag_ref[0], dense_ref, [peers, passed, pairs], None, window, None, sems, first=2)
    prior.start()
    result[...] = slots.sum_into(total, prior).astype(jnp.bfloat16)
    out = pltpu.make_async_copy(result, out_ref.at[:, there], out_sem)
    out.start()
    out.wait()


def shards(base_currents, term_rows, term_owner, term_slot, inductance, block_cols):
    devices = lax.axis_size("row")
    me = lax.axis_index("row")
    seg_dev, width = base_currents.shape
    capacity = max(2, 2 * term_rows.shape[0] // devices)
    slots = devices * capacity
    rows_dev, count, block, _ = inductance.shape

    core, side = me % 2, (me // 2) % 2
    across = [(i, i ^ 2) for i in range(devices)]
    partner = [(i, i ^ 1) for i in range(devices)]
    relay = [(i, (i - 4 if i & 2 else i + 4) % devices) for i in range(devices)]

    def send(value, pairs):
        return lax.ppermute(value, "row", pairs)

    near = jnp.where(core == 0, 4, 1)
    far = jnp.where(core == 0, 1, 4)
    slot_of = jnp.stack(
        [
            jnp.where(side == 0, 3, 2),
            near,
            jnp.zeros_like(near),
            far,
            jnp.where(side == 0, 2, 3),
            (me - HALO) * rows_dev,
        ]
    ).astype(jnp.int32)
    flag = jnp.stack([core == side, core != side]).astype(jnp.int32)

    outgoing = pl.pallas_call(
        functools.partial(pack_kernel, capacity),
        out_shape=pltpu.HBM((slots, width + LANES), jnp.bfloat16),
        in_specs=[HBM] * 3,
        out_specs=HBM,
        scratch_shapes=[
            pltpu.VMEM((1, term_rows.shape[0]), jnp.int32),
            pltpu.VMEM((1, term_rows.shape[0]), jnp.int32),
            pltpu.VMEM(term_rows.shape, jnp.bfloat16),
            pltpu.VMEM((slots, width + LANES), jnp.bfloat16),
            pltpu.SemaphoreType.DMA((3,)),
            pltpu.SemaphoreType.DMA((3,)),
        ],
        compiler_params=limit(16),
        name="pack_terms",
    )(*[in_hbm(item) for item in (term_owner.reshape(1, -1), term_slot.reshape(1, -1), term_rows)])
    arrived = lax.all_to_all(
        outgoing.reshape(devices, capacity, width + LANES), "row", split_axis=0, concat_axis=0, tiled=True
    ).reshape(slots, width + LANES)

    dense, dense_token = pl.pallas_call(
        dense_kernel,
        out_shape=(pltpu.HBM((seg_dev, SLOTS * seg_dev), jnp.bfloat16), TOKEN),
        grid=(rows_dev,),
        in_specs=[SMEM, SMEM, pl.BlockSpec((1, count, block, block), lambda r: (r, 0, 0, 0)), HBM],
        out_specs=(pl.BlockSpec((block, SLOTS * seg_dev), lambda r: (r, 0)), pl.BlockSpec(TOKEN.shape, lambda r: (0, 0))),
        scratch_shapes=[pltpu.VMEM((SLOTS * rows_dev, block, block), jnp.float32)],
        compiler_params=limit(24),
        cost_estimate=pl.CostEstimate(flops=0, bytes_accessed=0, transcendentals=0),
        name="dense_blocks",
    )(block_cols, slot_of, in_hbm(inductance), in_hbm(outgoing))


    sizes = chunk_sizes(width)
    starts = [sum(sizes[:k]) for k in range(len(sizes))]
    whole, *currents = pl.pallas_call(
        inject_kernel,
        out_shape=[
            jax.ShapeDtypeStruct((seg_dev, wide), jnp.bfloat16) for wide in [width] + sizes
        ],
        in_specs=[VMEM, VMEM, ANY],
        out_specs=[VMEM] * (1 + len(sizes)),
        compiler_params=limit(24),
        name="inject_terms",
    )(base_currents, arrived, dense_token)

    def cost():
        return pl.CostEstimate(flops=0, bytes_accessed=0, transcendentals=0)

    beside = send(whole, partner)
    peers = [send(current, across) for current in currents]

    passed = [send(peer, relay) for peer in peers]

    half = 2
    out_type = pltpu.HBM((seg_dev, width), jnp.bfloat16)

    across_beside = [send(peer, partner) for peer in peers]
    passed_beside = [send(item, partner) for item in passed[:-1]]
    sign = passed[half][:16, :LANES]
    for _ in range(3):
        sign = gate(sign, flag)

    wide = sum(sizes[:half])
    given = [dense, whole, beside] + peers[:half] + passed[:half]
    given += across_beside[:half] + passed_beside[:half]
    out, token = pl.pallas_call(
        functools.partial(flux_kernel, 0, half),
        out_shape=(out_type, TOKEN),
        in_specs=[SMEM] + [HBM] * len(given) + [ANY],
        out_specs=(HBM, VMEM),
        scratch_shapes=[
            pltpu.VMEM((SLOTS, seg_dev, seg_dev), jnp.bfloat16),
            pltpu.VMEM((SLOTS, seg_dev, wide), jnp.bfloat16),
            pltpu.VMEM((seg_dev, wide), jnp.float32),
            pltpu.VMEM((seg_dev, wide), jnp.bfloat16),
            pltpu.SemaphoreType.DMA((SLOTS,)),
            pltpu.SemaphoreType.DMA((SLOTS, half)),
            pltpu.SemaphoreType.DMA,
        ],
        compiler_params=limit(28),
        cost_estimate=cost(),
        name="flux",
    )(flag, *[in_hbm(item) for item in given], sign)

    rest, left = width - wide, len(sizes) - half
    sums, token = pl.pallas_call(
        functools.partial(near_kernel, wide),
        out_shape=(jax.ShapeDtypeStruct((seg_dev, rest), jnp.float32), TOKEN),
        in_specs=[VMEM, HBM, HBM, ANY],
        out_specs=(VMEM, VMEM),
        scratch_shapes=[
            pltpu.VMEM((2, seg_dev, rest), jnp.bfloat16),
            pltpu.SemaphoreType.DMA((2, 1)),
        ],
        compiler_params=limit(16),
        cost_estimate=cost(),
        name="near_flux",
    )(dense, in_hbm(whole), in_hbm(beside), token)
    passed[-1] = gate(passed[-1], token)
    passed_beside.append(send(passed[-1], partner))
    given = peers[half:] + passed[half:] + across_beside[half:] + passed_beside[half:]
    return pl.pallas_call(
        functools.partial(far_kernel, wide, left),
        out_shape=out_type,
        in_specs=[SMEM, VMEM] + [ANY] * (1 + len(given)) + [HBM],
        out_specs=HBM,
        scratch_shapes=[
            pltpu.VMEM((3, seg_dev, rest), jnp.bfloat16),
            pltpu.VMEM((seg_dev, rest), jnp.float32),
            pltpu.VMEM((seg_dev, rest), jnp.bfloat16),
            pltpu.SemaphoreType.DMA((3, left)),
            pltpu.SemaphoreType.DMA,
            pltpu.SemaphoreType.DMA,
        ],
        input_output_aliases={3 + len(given): 0},
        compiler_params=limit(16),
        cost_estimate=cost(),
        name="far_flux",
    )(flag, dense, sums, *given, in_hbm(out))


def solution(mesh):
    placed = (
        P(("group", "row"), None),
        P(("group", "row"), None),
        P(("group", "row"), None),
        P(("group", "row"), None),
        P("row", None, None, None),
        P("row", None),
    )
    return jax.shard_map(
        shards, mesh=mesh, in_specs=placed, out_specs=P(("group", "row"), None), check_vma=False
    )
```
